256 devices in a mesh: dp: 16 (over z_hi, x, core), tensor: 16 (over z_lo, y).
Axes of the slice: x: 4, y: 4, z: 8 (z_hi: 2, z_lo: 4; z = z_hi * 4 + z_lo), core: 2. Of those that a mesh axis runs over, the one named last changes fastest.
Arguments:
- inputs: bfloat16 [6144, 2560], P(('dp', 'tensor')), may hold values from -6 to 6
- norm_gain: float32 [2560], replicated, may hold values from 0.5 to 1.5
- w_up: bfloat16 [2560, 10240], P(None, 'tensor'), may hold values from -0.07905694 to 0.07905694
- w_down: bfloat16 [10240, 2560], P('tensor'), may hold values from -0.0625 to 0.0625
- grad_out: bfloat16 [6144, 2560], P(('dp', 'tensor')), may hold values from -7 to 7
Outputs:
- output: bfloat16 [6144, 2560], P(('dp', 'tensor'))
- grad_in: bfloat16 [6144, 2560], P(('dp', 'tensor'))
- grad_up: bfloat16 [2560, 10240], P(None, 'tensor')
- grad_down: bfloat16 [10240, 2560], P('tensor')
- grad_gain: float32 [2560], replicated
The draws below stay inside these ranges and needn't reach their ends.
All inputs are finite; a program needn't handle non-finite values.
Results may differ from the reference program's by a relative error of at most 0.024.
Values may be sent and summed in bfloat16 or wider, within the bound.
A program may use at most 192 MiB of HBM per device.

```python
import math
import jax
import jax.numpy as jnp
from jax import lax

D = 2560
FF = 10240
BLOCK = 16
TOK_GROUP = 384
TOKENS = 6144
N_DP = 16


def draw_w_up(key, part):
    key = jax.random.fold_in(key, 11)
    column = jnp.arange(FF, dtype=jnp.float32) / FF
    base_noise = jax.random.truncated_normal(key, -4.0, 4.0, (D, FF), jnp.float32)
    col_scale = jnp.exp(math.log(3.0) * (column - 1.0))
    return (base_noise * col_scale[None, :] * D ** (-0.5)).astype(jnp.bfloat16)


def draw_grad_out(key, part):
    key = jax.random.fold_in(key, 23)
    position = jnp.arange(TOKENS, dtype=jnp.float32) / TOKENS
    base_noise = jax.random.truncated_normal(key, -4.0, 4.0, (TOKENS, D), jnp.float32)
    row_scale = jnp.exp(math.log(3.0) * (position - 0.5))
    return (base_noise * row_scale[:, None]).astype(jnp.bfloat16)


def levels(own_key, dims, cuts, smallest, high):
    level, own = 1.0, jax.random.fold_in(own_key, 6)
    for dim, shards_of in cuts:
        draws = jnp.exp(jax.random.uniform(jax.random.fold_in(own, dim), (shards_of,), jnp.float32, smallest / len(cuts), high / len(cuts)))
        level = level * jnp.repeat(draws, dims[dim] // shards_of).reshape([-1 if axis == dim else 1 for axis in range(len(dims))])
    return level


def gaussian(rng, extent, deviation, reach, split=(), kind=jnp.bfloat16):
    entries = jax.random.normal(rng, extent, jnp.float32) * deviation
    if len(split) > 0:
        entries = levels(rng, extent, split, -0.22, 0.18) * entries
    return jnp.clip(entries, min=-reach, max=reach).astype(kind)


def setup_inputs(seed: int = 0) -> dict:
    keys = jax.random.split(jax.random.key(seed), 6)
    inputs = gaussian(keys[0], (TOKENS, D), 1.0, 6.0, ((0, 256),))
    norm_gain = jnp.clip(1.0 + 0.1 * jax.random.normal(keys[1], (D,), jnp.float32), 0.5, 1.5)
    w_up = draw_w_up(jax.random.fold_in(keys[5], 71), 0)
    w_down = gaussian(keys[3], (FF, D), FF ** -0.5, 0.0625, ((0, 16),))
    grad_out = draw_grad_out(jax.random.fold_in(keys[5], 71), 0)
    return {"inputs": inputs, "norm_gain": norm_gain, "w_up": w_up, "w_down": w_down, "grad_out": grad_out}


TWO_PI = 2.0 * math.pi
CONTRACT_ROWS = (((0,), (0,)), ((), ()))
CONTRACT_COLS = (((1,), (1,)), ((), ()))

def staircase(values):
    return values - jnp.sin(TWO_PI * values) / TWO_PI

def block_peak(values):
    row_count, col_count = values.shape
    block_max = lax.optimization_barrier(jnp.max(jnp.abs(values).reshape(row_count, col_count // BLOCK, BLOCK), axis=2))
    return jnp.repeat(block_max, BLOCK, axis=1)

def reference(inputs, norm_gain, w_up, w_down, grad_out):
    grouped = inputs.reshape(N_DP, TOK_GROUP, D)
    cot_grouped = grad_out.reshape(N_DP, TOK_GROUP, D)
    initial = (jnp.zeros((D, FF), jnp.float32), jnp.zeros((FF, D), jnp.float32), jnp.zeros((D,), jnp.float32))

    def one_group(carry, pair):
        up_total, down_total, gain_total = carry
        group_in, group_cot = pair
        widened = group_in.astype(jnp.float32)
        inverse = lax.rsqrt(lax.optimization_barrier(jnp.mean(widened * widened, axis=1, keepdims=True)) + 1e-05)
        normed = widened * inverse * norm_gain
        x_scale = jnp.maximum(block_peak(normed), 1.5) / 6.0
        quantized = (x_scale * staircase(normed / x_scale)).astype(jnp.bfloat16)
        pre_act = jnp.dot(quantized, w_up, preferred_element_type=jnp.float32)
        active = jnp.maximum(pre_act, 0.0)
        hidden = active * active
        peak_value = jnp.max(hidden) + 1e-06
        h_scale = jnp.maximum(block_peak(hidden), peak_value / 8.0) / 6.0
        hidden_q = (h_scale * staircase(hidden / h_scale)).astype(jnp.bfloat16)
        output = jnp.dot(hidden_q, w_down, preferred_element_type=jnp.float32).astype(jnp.bfloat16)
        grad_hq = lax.dot_general(group_cot, w_down, CONTRACT_COLS, preferred_element_type=jnp.float32)
        grad_z = (grad_hq * 2.0 * active).astype(jnp.bfloat16)
        grad_xq = lax.dot_general(grad_z, w_up, CONTRACT_COLS, preferred_element_type=jnp.float32)
        gain_total = gain_total + lax.optimization_barrier(jnp.sum(grad_xq * widened * inverse, axis=0))
        scaled = grad_xq * norm_gain
        cubed = inverse * inverse * inverse
        grad_rows = inverse * scaled - widened * cubed * lax.optimization_barrier(jnp.mean(scaled * widened, axis=1, keepdims=True))
        down_part = lax.dot_general(hidden_q, group_cot, CONTRACT_ROWS, preferred_element_type=jnp.float32)
        up_part = lax.dot_general(quantized, grad_z, CONTRACT_ROWS, preferred_element_type=jnp.float32)
        down_total = down_total + lax.optimization_barrier(down_part.astype(jnp.bfloat16)).astype(jnp.float32)
        up_total = up_total + lax.optimization_barrier(up_part.astype(jnp.bfloat16)).astype(jnp.float32)
        return ((up_total, down_total, gain_total), (output, grad_rows.astype(jnp.bfloat16)))
    finals, stacked = lax.scan(one_group, initial, (grouped, cot_grouped))
    up_total, down_total, gain_total = finals
    outputs, grads = stacked
    return (outputs.reshape(TOKENS, D), grads.reshape(TOKENS, D), up_total.astype(jnp.bfloat16), down_total.astype(jnp.bfloat16), gain_total)
```

```python
import functools

import jax
import jax.numpy as jnp
from jax import lax
from jax.experimental import pallas as pl
from jax.experimental.pallas import tpu as pltpu
from jax.sharding import PartitionSpec as P

MESH = pl.DeviceIdType.MESH
F32 = jnp.float32
BF16 = jnp.bfloat16

D = 2560
F = 640
T = 384
R = 24
H = D // 2
N_SEM = 256

SINE = (
    0.9999999958410793,
    -6.579735564529717,
    12.987846451008128,
    -12.207473944175224,
    6.687349899038311,
    -2.367236060103434,
    0.5102235956366108,
)
NT = (((1,), (1,)), ((), ()))
NN = (((1,), (0,)), ((), ()))


def dot(a, b, dims=NN):
    return lax.dot_general(a, b, dims, preferred_element_type=F32)


def staircase(values):
    r = values - jnp.floor(values + 0.5)
    s = r * r
    p = jnp.full_like(s, SINE[-1])
    for c in SINE[-2::-1]:
        p = p * s + c
    return values - p * r


def block_peak(values):
    lane = lax.broadcasted_iota(jnp.int32, values.shape, 1)
    for s in (1, 2, 4, 8):
        up = pltpu.roll(values, s, 1)
        down = pltpu.roll(values, 128 - s, 1)
        values = jnp.maximum(values, jnp.where((lane & s) != 0, up, down))
    return values


def quantize(values, magnitude, floor):
    peak = jnp.maximum(block_peak(magnitude), floor)
    return peak * (1.0 / 6.0) * staircase(values * (6.0 / peak))


class Copies:
    def __init__(self, send, recv):
        self.send, self.recv, self.all = send, recv, []

    def start(self, src, dst, device):
        n = len(self.all)
        copy = pltpu.make_async_remote_copy(
            src_ref=src,
            dst_ref=dst,
            send_sem=self.send.at[n],
            recv_sem=self.recv.at[n],
            device_id=device,
            device_id_type=MESH,
        )
        copy.start()
        self.all.append(copy)
        return copy


def kernel(
    x_ref, gain_ref, wu_hbm, wd_hbm, go_ref,
    out_ref, gin_ref, gup_ref, gdn_ref, gg_ref,
    wu, wd, cg, qg, c2, q2, aa, ss, cc, ghq, pa, gz2, hq, ht,
    po, px, ro, rx, zo, zx, u, ur, uz, d, dr, dz,
    py, pz, gy, gzl, gx, gc, gh, gfull, send, recv, local,
):
    dp, tn = lax.axis_index("dp"), lax.axis_index("tensor")
    zh, x, c = dp // 8, (dp // 2) % 4, dp % 2
    zl, y = tn // 4, tn % 4

    def dev(zh=zh, x=x, c=c, zl=zl, y=y):
        return ((zh * 4 + x) * 2 + c, zl * 4 + y)

    def mod(v):
        return lax.rem(v + 8, 4)

    def block(yy, zz):
        return yy * 4 + zz

    yp, ym = dev(y=mod(y + 1)), dev(y=mod(y - 1))
    xp, xm = dev(x=mod(x + 1)), dev(x=mod(x - 1))
    other = dev(c=1 - c)
    zfar = dev(zh=1 - zh)
    y_peers = [dev(y=mod(y + k)) for k in (1, 2, 3)]
    z_peers = [dev(zl=mod(zl + k)) for k in (1, 2, 3)]
    x_peers = [dev(x=mod(x + k)) for k in (1, 2, 3)]
    copies = Copies(send, recv)
    go = copies.start

    load_up = pltpu.make_async_copy(wu_hbm, wu, local.at[0])
    load_up.start()
    load_down = pltpu.make_async_copy(wd_hbm, wd, local.at[1])
    load_down.start()

    barrier = pltpu.get_barrier_semaphore()
    peers = y_peers + z_peers + x_peers + [other, zfar]
    for peer in peers:
        pl.semaphore_signal(barrier, inc=1, device_id=peer, device_id_type=MESH)
    pl.semaphore_wait(barrier, len(peers))

    def gather_z(buf, src):
        at = buf.at[block(y, zl)]
        return [go(src, at, peer) for peer in z_peers]

    def gather_y(buf, k, src=None):
        at = buf.at[block(y, mod(zl - k))]
        src = at if src is None else src
        return go(src, at, yp), go(src, at, ym)

    def forward(buf, k, pair):
        plus, minus = pair
        zz = mod(zl - k)
        plus.wait_recv()
        at = buf.at[block(mod(y - 1), zz), :, pl.ds(0, H)]
        a = go(at, at, yp)
        minus.wait_recv()
        at = buf.at[block(mod(y + 1), zz), :, pl.ds(H, H)]
        b = go(at, at, ym)
        return a, b

    cz = gather_z(cg, go_ref)
    cy = [gather_y(cg, 0, go_ref)]
    cg[block(y, zl)] = go_ref[...]

    wide = x_ref[...].astype(F32)
    inverse = lax.rsqrt(jnp.mean(wide * wide, axis=1, keepdims=True) + 1e-05)
    for i in range(D // 128):
        cols = slice(i * 128, (i + 1) * 128)
        normed = wide[:, cols] * inverse * gain_ref[:, cols]
        q = quantize(normed, jnp.abs(normed), 1.5)
        qg[block(y, zl), :, cols] = q.astype(BF16)

    qz = gather_z(qg, qg.at[block(y, zl)])
    qy = [gather_y(qg, 0)]
    for k in (1, 2, 3):
        cz[k - 1].wait_recv()
        cy.append(gather_y(cg, k))
    cf = [forward(cg, k, cy[k]) for k in (0, 1)]
    for k in (1, 2, 3):
        qz[k - 1].wait_recv()
        qy.append(gather_y(qg, k))
    cf += [forward(cg, k, cy[k]) for k in (2, 3)]
    qf = [forward(qg, k, qy[k]) for k in (0, 1)]
    for pair in cf:
        for copy in pair:
            copy.wait_recv()

    @pl.loop(0, D // 256)
    def _(i):
        cols = pl.ds(pl.multiple_of(i * 256, 256), 256)
        c2[:, cols] = cg[:, :, cols].astype(F32).reshape(T, 256).astype(BF16)

    other_half = pl.ds(pl.multiple_of((1 - c) * H, H), H)
    own_half = pl.ds(pl.multiple_of(c * H, H), H)
    ccx = go(c2.at[:, other_half], cc.at[pl.ds(T, T), :], other)
    cc[pl.ds(0, T), :] = c2[:, own_half]

    qf += [forward(qg, k, qy[k]) for k in (2,)]
    load_down.wait()

    @pl.loop(0, 5)
    def _(i):
        ks = pl.ds(pl.multiple_of(i * 512, 512), 512)
        part = dot(c2[:, ks], wd[:, ks], NT)

        @pl.when(i == 0)
        def _():
            ghq[...] = part

        @pl.when(i > 0)
        def _():
            ghq[...] += part

    qf += [forward(qg, k, qy[k]) for k in (3,)]
    for pair in qf:
        for copy in pair:
            copy.wait_recv()

    def lay(i, start, put):
        cols = pl.ds(pl.multiple_of(start + i * 256, 256), 256)
        v = qg[:, :, cols].astype(F32).reshape(T, 256)
        q2[:, cols] = v.astype(BF16)
        put(pl.ds(pl.multiple_of(i * 256, 256), 256), v.T.astype(BF16))

    def put_other(rows, v):
        ss[rows, :] = v

    def put_own(rows, v):
        aa[rows, pl.ds(0, T)] = v

    @pl.loop(0, 5)
    def _(i):
        lay(i, (1 - c) * H, put_other)

    aax = go(ss, aa.at[:, pl.ds(T, T)], other)

    @pl.loop(0, 5)
    def _(i):
        lay(i, c * H, put_own)

    load_up.wait()

    @pl.loop(0, 5)
    def _(i):
        ks = pl.ds(pl.multiple_of(i * 512, 512), 512)
        part = dot(q2[:, ks], wu[ks, :])

        @pl.when(i == 0)
        def _():
            pa[...] = part

        @pl.when(i > 0)
        def _():
            pa[...] += part

    def grad_tile(i, most):
        rows = pl.ds(pl.multiple_of(i * 64, 64), 64)
        for j in range(F // 128):
            cols = slice(j * 128, (j + 1) * 128)
            active = jnp.maximum(pa[rows, cols], 0.0)
            pa[rows, cols] = active
            gz2[rows, cols] = (ghq[rows, cols] * 2.0 * active).astype(BF16)
            most = jnp.maximum(most, active)
        return most

    most = lax.fori_loop(0, T // 64, grad_tile, jnp.zeros((64, 128), F32))
    gzx = go(gz2.at[pl.ds(0, T)], gz2.at[pl.ds(T, T)], other)
    most = jnp.max(jnp.max(most, axis=0, keepdims=True), axis=1, keepdims=True)
    py[y] = jnp.broadcast_to(most * most, (8, 128))
    pyx = [go(py.at[y], py.at[y], peer) for peer in y_peers]

    class Ring:
        def __init__(self, pos, plus, minus, view, got, add):
            self.pos, self.to = pos, (plus, minus)
            self.view, self.got, self.add = view, got, add
            self.last = [None, None]

        def send(self, s, way):
            j = mod(self.pos - 1 - s) if way == 0 else mod(self.pos + 1 + s)
            at = self.view(j, way)
            self.last[way] = go(at, self.got.at[way, s], self.to[way])

        def take(self, s):
            for way in (0, 1):
                self.last[way].wait_recv()
                j = mod(self.pos - 2 - s) if way == 0 else mod(self.pos + 2 + s)
                self.add(j, way, s)
                if s < 2:
                    self.send(s + 1, way)

    def adder(view, got, tiles, cut):
        def add(j, way, s):
            mine, theirs = view(j, way), got.at[way, s]

            @pl.loop(0, tiles)
            def _(i):
                at = cut(i)
                mine[at] = (mine[at].astype(F32) + theirs[at].astype(F32)).astype(BF16)

        return add

    def rows_of(n):
        return lambda i: (pl.ds(pl.multiple_of(i * n, n), n), slice(None))

    def u_view(j, way):
        return u.at[j, way]

    def d_view(j, way):
        return d.at[j, way]

    def p_view(buf):
        return lambda j, way: buf.at[j, :, :, pl.ds(way * H, H)]

    up = Ring(x, xp, xm, u_view, ur, adder(u_view, ur, 5, rows_of(32)))
    down = Ring(x, xp, xm, d_view, dr, adder(d_view, dr, 5, rows_of(16)))
    out = Ring(y, yp, ym, p_view(po), ro, adder(p_view(po), ro, 4, lambda i: i))
    gin = Ring(y, yp, ym, p_view(px), rx, adder(p_view(px), rx, 4, lambda i: i))

    aax.wait_recv()
    gzx.wait_recv()

    def up_chunk(j):
        rows = pl.ds(pl.multiple_of(j * 320, 320), 320)
        u[j] = dot(aa[rows, :], gz2[...]).reshape(2, 160, F).astype(BF16)

    up_chunk(mod(x - 1))
    up.send(0, 0)
    up_chunk(mod(x + 1))
    up.send(0, 1)
    up_chunk(mod(x + 2))
    up_chunk(x)

    for copy in pyx:
        copy.wait_recv()
    peak = jnp.maximum(jnp.maximum(py[0], py[1]), jnp.maximum(py[2], py[3]))
    pz[zl] = peak
    pzx = [go(pz.at[zl], pz.at[zl], peer) for peer in z_peers]

    @pl.loop(0, 5)
    def _(i):
        ns = pl.ds(pl.multiple_of(i * 512, 512), 512)
        part = dot(gz2[pl.ds(0, T), :], wu[ns, :], NT)
        px[:, :, :, ns] = part.reshape(4, 4, R, 512).astype(BF16)

    gin.send(0, 0)
    gin.send(0, 1)

    for copy in pzx:
        copy.wait_recv()
    peak = jnp.maximum(jnp.maximum(pz[0], pz[1]), jnp.maximum(pz[2], pz[3]))
    floor = (peak[0:1, :] + 1e-06) * 0.125

    @pl.loop(0, T // 128)
    def _(i):
        rows = pl.ds(pl.multiple_of(i * 128, 128), 128)
        for j in range(F // 128):
            cols = slice(j * 128, (j + 1) * 128)
            active = pa[rows, cols]
            hidden = active * active
            q = quantize(hidden, hidden, floor)
            hq[rows, cols] = q.astype(BF16)
            ht[cols, rows] = q.T.astype(BF16)

    htx = go(ht.at[:, pl.ds(0, T)], ht.at[:, pl.ds(T, T)], other)
    up.take(0)

    @pl.loop(0, 5)
    def _(i):
        ns = pl.ds(pl.multiple_of(i * 512, 512), 512)
        part = dot(hq[...], wd[:, ns])
        po[:, :, :, ns] = part.reshape(4, 4, R, 512).astype(BF16)

    ccx.wait_recv()
    htx.wait_recv()

    def down_chunk(j):
        rows = pl.ds(pl.multiple_of(j * 160, 160), 160)
        d[j] = dot(ht[rows, :], cc[...]).reshape(2, 80, H).astype(BF16)

    down_chunk(mod(x - 1))
    down.send(0, 0)
    down_chunk(mod(x + 1))
    down.send(0, 1)
    out.send(0, 0)
    out.send(0, 1)
    down_chunk(mod(x + 2))
    down_chunk(x)

    gin.take(0)
    up.take(1)
    down.take(0)
    out.take(0)
    up.take(2)
    uzx = go(u.at[x], uz, zfar)
    gin.take(1)
    down.take(1)
    out.take(1)
    gin.take(2)

    def scatter_z(buf, got):
        return [
            go(buf.at[y, mod(zl + k)], got.at[k - 1], z_peers[k - 1]) for k in (1, 2, 3)
        ]

    gin_z = scatter_z(px, zx)
    down.take(2)
    dzx = go(d.at[x], dz, zfar)
    out.take(2)
    out_z = scatter_z(po, zo)

    for copy in gin_z:
        copy.wait_recv()

    def total(buf, got, cols):
        t = buf[y, zl, :, cols].astype(F32) + got[0, :, cols].astype(F32)
        return t + got[1, :, cols].astype(F32) + got[2, :, cols].astype(F32)

    dots = jnp.zeros((R, 128), F32)
    for i in range(D // 128):
        cols = slice(i * 128, (i + 1) * 128)
        g = total(px, zx, cols)
        w = x_ref[:, cols].astype(F32)
        gfull[:, cols] = g
        dots = dots + g * gain_ref[:, cols] * w
        gy[y, i : i + 1, :] = jnp.sum(g * w * inverse, axis=0, keepdims=True)
    gyx = [go(gy.at[y], gy.at[y], peer) for peer in y_peers]
    mean = jnp.sum(dots, axis=1, keepdims=True) * (1.0 / D)
    cubed = inverse * inverse * inverse * mean
    for i in range(D // 128):
        cols = slice(i * 128, (i + 1) * 128)
        w = x_ref[:, cols].astype(F32)
        gin_ref[:, cols] = (
            inverse * (gfull[:, cols] * gain_ref[:, cols]) - w * cubed
        ).astype(BF16)

    for copy in gyx:
        copy.wait_recv()
    gzl[zl] = gy[0] + gy[1] + gy[2] + gy[3]
    gzx2 = [go(gzl.at[zl], gzl.at[zl], peer) for peer in z_peers]

    def spread(own, chunk, buf, at_chunk, at_half):
        res = []
        at = buf.at[at_chunk(c, x)]
        res.append((go(at, at, xp), go(at, at, xm)))
        res.append(go(at, at, other))
        return res

    def up_rows(cc_, j, way=None):
        if way is None:
            return (pl.ds(pl.multiple_of(cc_ * H + j * 320, 320), 320), slice(None))
        start = cc_ * H + j * 320 + way * 160
        return (pl.ds(pl.multiple_of(start, 160), 160), slice(None))

    def down_rows(cc_, j, way=None):
        cols = pl.ds(pl.multiple_of(cc_ * H, H), H)
        if way is None:
            return (pl.ds(pl.multiple_of(j * 160, 160), 160), cols)
        return (pl.ds(pl.multiple_of(j * 160 + way * 80, 80), 80), cols)

    class Spread:
        def __init__(self, buf, where):
            self.buf, self.where = buf, where

        def begin(self):
            at = self.buf.at[self.where(c, x)]
            self.plus, self.minus = go(at, at, xp), go(at, at, xm)
            self.cross = [go(at, at, other)]

        def middle(self):
            self.plus.wait_recv()
            at = self.buf.at[self.where(c, mod(x - 1), 0)]
            self.fplus = go(at, at, xp)
            at = self.buf.at[self.where(c, mod(x - 1))]
            self.cross.append(go(at, at, other))
            self.minus.wait_recv()
            at = self.buf.at[self.where(c, mod(x + 1), 1)]
            self.fminus = go(at, at, xm)
            at = self.buf.at[self.where(c, mod(x + 1))]
            self.cross.append(go(at, at, other))

        def end(self):
            self.fplus.wait_recv()
            at = self.buf.at[self.where(c, mod(x + 2), 0)]
            self.cross.append(go(at, at, other))
            self.fminus.wait_recv()
            at = self.buf.at[self.where(c, mod(x + 2), 1)]
            self.cross.append(go(at, at, other))

        def finish(self):
            for copy in self.cross:
                copy.wait_recv()

    uzx.wait_recv()
    for way in (0, 1):
        gup_ref[up_rows(c, x, way)] = (
            u[x, way].astype(F32) + uz[way].astype(F32)
        ).astype(BF16)
    spread_up = Spread(gup_ref, up_rows)
    spread_up.begin()

    for copy in gzx2:
        copy.wait_recv()
    gx[x] = gzl[0] + gzl[1] + gzl[2] + gzl[3]
    gxx = [go(gx.at[x], gx.at[x], peer) for peer in x_peers]

    for copy in out_z:
        copy.wait_recv()
    for i in range(D // 128):
        cols = slice(i * 128, (i + 1) * 128)
        out_ref[:, cols] = total(po, zo, cols).astype(BF16)

    spread_up.middle()

    for copy in gxx:
        copy.wait_recv()
    gc[c] = gx[0] + gx[1] + gx[2] + gx[3]
    gcx = go(gc.at[c], gc.at[c], other)

    dzx.wait_recv()
    for way in (0, 1):
        gdn_ref[down_rows(c, x, way)] = (
            d[x, way].astype(F32) + dz[way].astype(F32)
        ).astype(BF16)
    spread_down = Spread(gdn_ref, down_rows)
    spread_down.begin()

    gcx.wait_recv()
    gh[zh] = gc[0] + gc[1]
    ghx = go(gh.at[zh], gh.at[zh], zfar)
    spread_up.end()
    ghx.wait_recv()
    gg_ref[...] = gh[0] + gh[1]
    spread_down.middle()
    spread_down.end()
    spread_up.finish()
    spread_down.finish()
    for copy in copies.all:
        copy.wait_send()
    assert len(copies.all) <= N_SEM, len(copies.all)


def per_device(inputs, norm_gain, w_up, w_down, grad_out):
    vmem = pl.BlockSpec(memory_space=pltpu.VMEM)
    hbm = pl.BlockSpec(memory_space=pl.ANY)
    scratch = [
        ((D, F), BF16), ((F, D), BF16),
        ((16, R, D), BF16), ((16, R, D), BF16),
        ((T, D), BF16), ((T, D), BF16),
        ((H, 2 * T), BF16), ((H, T), BF16), ((2 * T, H), BF16),
        ((T, F), F32), ((T, F), F32),
        ((2 * T, F), BF16), ((T, F), BF16), ((F, 2 * T), BF16),
        ((4, 4, R, D), BF16), ((4, 4, R, D), BF16),
        ((2, 3, 4, R, H), BF16), ((2, 3, 4, R, H), BF16),
        ((3, R, D), BF16), ((3, R, D), BF16),
        ((4, 2, 160, F), BF16), ((2, 3, 160, F), BF16), ((2, 160, F), BF16),
        ((4, 2, 80, H), BF16), ((2, 3, 80, H), BF16), ((2, 80, H), BF16),
        ((4, 8, 128), F32), ((4, 8, 128), F32),
        ((4, 20, 128), F32), ((4, 20, 128), F32), ((4, 20, 128), F32),
        ((2, 20, 128), F32), ((2, 20, 128), F32),
        ((R, D), F32),
    ]
    out, gin, gup, gdn, gg = pl.pallas_call(
        kernel,
        out_shape=(
            jax.ShapeDtypeStruct((R, D), BF16),
            jax.ShapeDtypeStruct((R, D), BF16),
            jax.ShapeDtypeStruct((D, F), BF16),
            jax.ShapeDtypeStruct((F, D), BF16),
            jax.ShapeDtypeStruct((D // 128, 128), F32),
        ),
        in_specs=[vmem, vmem, hbm, hbm, vmem],
        out_specs=(vmem,) * 5,
        scratch_shapes=[pltpu.VMEM(s, t) for s, t in scratch]
        + [
            pltpu.SemaphoreType.DMA((N_SEM,)),
            pltpu.SemaphoreType.DMA((N_SEM,)),
            pltpu.SemaphoreType.DMA((2,)),
        ],
        compiler_params=pltpu.CompilerParams(
            collective_id=0, has_side_effects=True, vmem_limit_bytes=62 << 20
        ),
    )(inputs, norm_gain.reshape(1, D), w_up, w_down, grad_out)
    return out, gin, gup, gdn, gg.reshape(D)


def solution(mesh):
    return jax.shard_map(
        per_device,
        mesh=mesh,
        in_specs=(
            P(("dp", "tensor"), None),
            P(),
            P(None, "tensor"),
            P("tensor", None),
            P(("dp", "tensor"), None),
        ),
        out_specs=(
            P(("dp", "tensor"), None),
            P(("dp", "tensor"), None),
            P(None, "tensor"),
            P("tensor", None),
            P(),
        ),
        check_vma=False,
    )
```

```python
import functools

import jax
import jax.numpy as jnp
from jax import lax
from jax.experimental import pallas as pl
from jax.experimental.pallas import tpu as pltpu
from jax.sharding import PartitionSpec as P

MESH = pl.DeviceIdType.MESH
F32 = jnp.float32
BF16 = jnp.bfloat16

D = 2560
F = 640
T = 384
R = 24
H = D // 2
N_SEM = 256

SINE = (
    0.9999999958410793,
    -6.579735564529717,
    12.987846451008128,
    -12.207473944175224,
    6.687349899038311,
    -2.367236060103434,
    0.5102235956366108,
)
NT = (((1,), (1,)), ((), ()))
NN = (((1,), (0,)), ((), ()))


def dot(a, b, dims=NN):
    return lax.dot_general(a, b, dims, preferred_element_type=F32)


def staircase(values):
    r = values - jnp.floor(values + 0.5)
    s = r * r
    p = jnp.full_like(s, SINE[-1])
    for c in SINE[-2::-1]:
        p = p * s + c
    return values - p * r


def block_peak(values):
    lane = lax.broadcasted_iota(jnp.int32, values.shape, 1)
    for s in (1, 2, 4, 8):
        up = pltpu.roll(values, s, 1)
        down = pltpu.roll(values, 128 - s, 1)
        values = jnp.maximum(values, jnp.where((lane & s) != 0, up, down))
    return values


def quantize(values, magnitude, floor):
    peak = jnp.maximum(block_peak(magnitude), floor)
    return peak * (1.0 / 6.0) * staircase(values * (6.0 / peak))


class Copies:
    def __init__(self, send, recv):
        self.send, self.recv, self.all = send, recv, []

    def start(self, src, dst, device):
        n = len(self.all)
        copy = pltpu.make_async_remote_copy(
            src_ref=src,
            dst_ref=dst,
            send_sem=self.send.at[n],
            recv_sem=self.recv.at[n],
            device_id=device,
            device_id_type=MESH,
        )
        copy.start()
        self.all.append(copy)
        return copy


def kernel(
    x_ref, gain_ref, wu_hbm, wd_hbm, go_ref,
    out_ref, gin_ref, gup_ref, gdn_ref, gg_ref,
    wu, wd, cg, qg, c2, q2, aa, ss, cc, ghq, pa, gz2, hq, ht,
    po, px, ro, rx, zo, zx, w, wr, wz,
    py, pz, gy, gzl, gx, gc, gh, gfull, send, recv, local,
):
    dp, tn = lax.axis_index("dp"), lax.axis_index("tensor")
    zh, x, c = dp // 8, (dp // 2) % 4, dp % 2
    zl, y = tn // 4, tn % 4

    def dev(zh=zh, x=x, c=c, zl=zl, y=y):
        return ((zh * 4 + x) * 2 + c, zl * 4 + y)

    def mod(v):
        return lax.rem(v + 8, 4)

    def block(yy, zz):
        return yy * 4 + zz

    yp, ym = dev(y=mod(y + 1)), dev(y=mod(y - 1))
    xp, xm = dev(x=mod(x + 1)), dev(x=mod(x - 1))
    other = dev(c=1 - c)
    zfar = dev(zh=1 - zh)
    y_peers = [dev(y=mod(y + k)) for k in (1, 2, 3)]
    z_peers = [dev(zl=mod(zl + k)) for k in (1, 2, 3)]
    x_peers = [dev(x=mod(x + k)) for k in (1, 2, 3)]
    copies = Copies(send, recv)
    go = copies.start

    load_up = pltpu.make_async_copy(wu_hbm, wu, local.at[0])
    load_up.start()
    load_down = pltpu.make_async_copy(wd_hbm, wd, local.at[1])
    load_down.start()

    barrier = pltpu.get_barrier_semaphore()
    peers = y_peers + z_peers + x_peers + [other, zfar]
    for peer in peers:
        pl.semaphore_signal(barrier, inc=1, device_id=peer, device_id_type=MESH)
    pl.semaphore_wait(barrier, len(peers))

    def gather_z(buf, src):
        at = buf.at[block(y, zl)]
        return [go(src, at, peer) for peer in z_peers]

    def gather_y(buf, k, src=None):
        at = buf.at[block(y, mod(zl - k))]
        src = at if src is None else src
        return go(src, at, yp), go(src, at, ym)

    def forward(buf, k, pair):
        plus, minus = pair
        zz = mod(zl - k)
        plus.wait_recv()
        at = buf.at[block(mod(y - 1), zz), :, pl.ds(0, H)]
        a = go(at, at, yp)
        minus.wait_recv()
        at = buf.at[block(mod(y + 1), zz), :, pl.ds(H, H)]
        b = go(at, at, ym)
        return a, b

    cz = gather_z(cg, go_ref)
    cy = [gather_y(cg, 0, go_ref)]
    cg[block(y, zl)] = go_ref[...]

    wide = x_ref[...].astype(F32)
    inverse = lax.rsqrt(jnp.mean(wide * wide, axis=1, keepdims=True) + 1e-05)
    for i in range(D // 128):
        cols = slice(i * 128, (i + 1) * 128)
        normed = wide[:, cols] * inverse * gain_ref[i : i + 1, :]
        q = quantize(normed, jnp.abs(normed), 1.5)
        qg[block(y, zl), :, cols] = q.astype(BF16)

    qz = gather_z(qg, qg.at[block(y, zl)])
    qy = [gather_y(qg, 0)]
    for k in (1, 2, 3):
        cz[k - 1].wait_recv()
        cy.append(gather_y(cg, k))
    cf = [forward(cg, k, cy[k]) for k in (0, 1)]
    for k in (1, 2, 3):
        qz[k - 1].wait_recv()
        qy.append(gather_y(qg, k))
    cf += [forward(cg, k, cy[k]) for k in (2, 3)]
    qf = [forward(qg, k, qy[k]) for k in (0, 1)]
    for pair in cf:
        for copy in pair:
            copy.wait_recv()

    @pl.loop(0, D // 256)
    def _(i):
        cols = pl.ds(pl.multiple_of(i * 256, 256), 256)
        c2[:, cols] = cg[:, :, cols].astype(F32).reshape(T, 256).astype(BF16)

    other_half = pl.ds(pl.multiple_of((1 - c) * H, H), H)
    own_half = pl.ds(pl.multiple_of(c * H, H), H)
    ccx = go(c2.at[:, other_half], cc.at[pl.ds(T, T), :], other)
    cc[pl.ds(0, T), :] = c2[:, own_half]

    qf += [forward(qg, k, qy[k]) for k in (2,)]
    load_down.wait()

    @pl.loop(0, 5)
    def _(i):
        ks = pl.ds(pl.multiple_of(i * 512, 512), 512)
        part = dot(c2[:, ks], wd[:, ks], NT)

        @pl.when(i == 0)
        def _():
            ghq[...] = part

        @pl.when(i > 0)
        def _():
            ghq[...] += part

    qf += [forward(qg, k, qy[k]) for k in (3,)]
    for pair in qf:
        for copy in pair:
            copy.wait_recv()

    def lay(i, start, put):
        cols = pl.ds(pl.multiple_of(start + i * 256, 256), 256)
        v = qg[:, :, cols].astype(F32).reshape(T, 256)
        q2[:, cols] = v.astype(BF16)
        put(pl.ds(pl.multiple_of(i * 256, 256), 256), v.T.astype(BF16))

    def put_other(rows, v):
        ss[rows, :] = v

    def put_own(rows, v):
        aa[rows, pl.ds(0, T)] = v

    @pl.loop(0, 5)
    def _(i):
        lay(i, (1 - c) * H, put_other)

    aax = go(ss, aa.at[:, pl.ds(T, T)], other)

    @pl.loop(0, 5)
    def _(i):
        lay(i, c * H, put_own)

    load_up.wait()

    @pl.loop(0, 5)
    def _(i):
        ks = pl.ds(pl.multiple_of(i * 512, 512), 512)
        part = dot(q2[:, ks], wu[ks, :])

        @pl.when(i == 0)
        def _():
            pa[...] = part

        @pl.when(i > 0)
        def _():
            pa[...] += part

    def grad_tile(i, most):
        rows = pl.ds(pl.multiple_of(i * 64, 64), 64)
        for j in range(F // 128):
            cols = slice(j * 128, (j + 1) * 128)
            active = jnp.maximum(pa[rows, cols], 0.0)
            pa[rows, cols] = active
            gz2[rows, cols] = (ghq[rows, cols] * 2.0 * active).astype(BF16)
            most = jnp.maximum(most, active)
        return most

    most = lax.fori_loop(0, T // 64, grad_tile, jnp.zeros((64, 128), F32))
    gzx = go(gz2.at[pl.ds(0, T)], gz2.at[pl.ds(T, T)], other)
    most = jnp.max(jnp.max(most, axis=0, keepdims=True), axis=1, keepdims=True)
    py[y] = jnp.broadcast_to(most * most, (8, 128))
    pyx = [go(py.at[y], py.at[y], peer) for peer in y_peers]

    class Ring:
        def __init__(self, pos, plus, minus, view, got, tiles, cut):
            self.pos, self.to = pos, (plus, minus)
            self.view, self.got, self.tiles, self.cut = view, got, tiles, cut
            self.last = [None, None]

        def send(self, s, way):
            j = mod(self.pos - 1 - s) if way == 0 else mod(self.pos + 1 + s)
            at = self.view(j, way)
            self.last[way] = go(at, self.got.at[way, s], self.to[way])

        def take(self, s):
            for way in (0, 1):
                self.last[way].wait_recv()
                j = mod(self.pos - 2 - s) if way == 0 else mod(self.pos + 2 + s)
                mine, theirs = self.view(j, way), self.got.at[way, s]

                @pl.loop(0, self.tiles)
                def _(i):
                    at = self.cut(i)
                    both = mine[at].astype(F32) + theirs[at].astype(F32)
                    mine[at] = both.astype(BF16)

                if s < 2:
                    self.send(s + 1, way)

    class Part:
        def __init__(self, n, buf, where):
            self.n, self.buf, self.where = n, buf, where
            self.ring = Ring(
                x, xp, xm, lambda j, way: w.at[n, j, way], wr.at[n], 5,
                lambda i: pl.ds(pl.multiple_of(i * 16, 16), 16),
            )

        def cross_z(self):
            self.far = go(w.at[self.n, x], wz.at[self.n], zfar)

        def begin(self):
            self.far.wait_recv()
            for way in (0, 1):
                both = w[self.n, x, way].astype(F32) + wz[self.n, way].astype(F32)
                self.buf[self.where(c, x, way)] = both.astype(BF16)
            at = self.buf.at[self.where(c, x)]
            self.plus, self.minus = go(at, at, xp), go(at, at, xm)
            self.cross = [go(at, at, other)]

        def middle(self):
            self.plus.wait_recv()
            at = self.buf.at[self.where(c, mod(x - 1), 0)]
            self.fplus = go(at, at, xp)
            at = self.buf.at[self.where(c, mod(x - 1))]
            self.cross.append(go(at, at, other))
            self.minus.wait_recv()
            at = self.buf.at[self.where(c, mod(x + 1), 1)]
            self.fminus = go(at, at, xm)
            at = self.buf.at[self.where(c, mod(x + 1))]
            self.cross.append(go(at, at, other))

        def end(self):
            self.fplus.wait_recv()
            at = self.buf.at[self.where(c, mod(x + 2), 0)]
            self.cross.append(go(at, at, other))
            self.fminus.wait_recv()
            at = self.buf.at[self.where(c, mod(x + 2), 1)]
            self.cross.append(go(at, at, other))

        def finish(self):
            for copy in self.cross:
                copy.wait_recv()

    def up_rows(p):
        def where(core, j, way=None):
            start = core * H + j * 320 + p * 160 + (0 if way is None else way * 80)
            n = 160 if way is None else 80
            return (pl.ds(pl.multiple_of(start, n), n), slice(None))

        return where

    def down_rows(p):
        def where(core, j, way=None):
            cols = pl.ds(pl.multiple_of(core * H + p * F, 128), F)
            start = j * 160 + (0 if way is None else way * 80)
            n = 160 if way is None else 80
            return (pl.ds(pl.multiple_of(start, n), n), cols)

        return where

    j1, j2 = Part(0, gup_ref, up_rows(0)), Part(1, gup_ref, up_rows(1))
    j3, j4 = Part(2, gdn_ref, down_rows(0)), Part(3, gdn_ref, down_rows(1))

    def p_view(buf):
        return lambda j, way: buf.at[j, :, :, pl.ds(way * H, H)]

    out = Ring(y, yp, ym, p_view(po), ro, 4, lambda i: i)
    gin = Ring(y, yp, ym, p_view(px), rx, 4, lambda i: i)

    aax.wait_recv()
    gzx.wait_recv()

    def up_chunk(p, j):
        rows = pl.ds(pl.multiple_of(j * 320 + p * 160, 160), 160)
        w[p, j] = dot(aa[rows, :], gz2[...]).reshape(2, 80, F).astype(BF16)

    for p, part in ((0, j1), (1, j2)):
        up_chunk(p, mod(x - 1))
        part.ring.send(0, 0)
        up_chunk(p, mod(x + 1))
        part.ring.send(0, 1)
    up_chunk(0, mod(x + 2))
    up_chunk(1, mod(x + 2))

    for copy in pyx:
        copy.wait_recv()
    peak = jnp.maximum(jnp.maximum(py[0], py[1]), jnp.maximum(py[2], py[3]))
    pz[zl] = peak
    pzx = [go(pz.at[zl], pz.at[zl], peer) for peer in z_peers]

    up_chunk(0, x)
    up_chunk(1, x)

    @pl.loop(0, 5)
    def _(i):
        ns = pl.ds(pl.multiple_of(i * 512, 512), 512)
        part = dot(gz2[pl.ds(0, T), :], wu[ns, :], NT)
        px[:, :, :, ns] = part.reshape(4, 4, R, 512).astype(BF16)

    j1.ring.take(0)
    gin.send(0, 0)
    gin.send(0, 1)
    j2.ring.take(0)

    for copy in pzx:
        copy.wait_recv()
    peak = jnp.maximum(jnp.maximum(pz[0], pz[1]), jnp.maximum(pz[2], pz[3]))
    floor = (peak[0:1, :] + 1e-06) * 0.125

    @pl.loop(0, T // 128)
    def _(i):
        rows = pl.ds(pl.multiple_of(i * 128, 128), 128)
        for j in range(F // 128):
            cols = slice(j * 128, (j + 1) * 128)
            active = pa[rows, cols]
            hidden = active * active
            q = quantize(hidden, hidden, floor)
            hq[rows, cols] = q.astype(BF16)
            ht[cols, rows] = q.T.astype(BF16)

    htx = go(ht.at[:, pl.ds(0, T)], ht.at[:, pl.ds(T, T)], other)
    j1.ring.take(1)
    j2.ring.take(1)
    gin.take(0)

    ccx.wait_recv()
    htx.wait_recv()

    def down_chunk(j):
        rows = pl.ds(pl.multiple_of(j * 160, 160), 160)
        for p in (0, 1):
            part = dot(ht[rows, :], cc[:, p * F : (p + 1) * F])
            w[2 + p, j] = part.reshape(2, 80, F).astype(BF16)

    down_chunk(mod(x - 1))
    j3.ring.send(0, 0)
    down_chunk(mod(x + 1))
    j3.ring.send(0, 1)
    j1.ring.take(2)
    j1.cross_z()
    j4.ring.send(0, 0)
    j4.ring.send(0, 1)
    down_chunk(mod(x + 2))
    j2.ring.take(2)
    j2.cross_z()
    down_chunk(x)

    @pl.loop(0, 5)
    def _(i):
        ns = pl.ds(pl.multiple_of(i * 512, 512), 512)
        part = dot(hq[...], wd[:, ns])
        po[:, :, :, ns] = part.reshape(4, 4, R, 512).astype(BF16)

    j3.ring.take(0)
    gin.take(1)
    out.send(0, 0)
    out.send(0, 1)
    j4.ring.take(0)

    def scatter_z(buf, got):
        return [
            go(buf.at[y, mod(zl + k)], got.at[k - 1], z_peers[k - 1]) for k in (1, 2, 3)
        ]

    j3.ring.take(1)
    gin.take(2)
    gin_z = scatter_z(px, zx)
    j4.ring.take(1)
    j1.begin()
    j3.ring.take(2)
    j3.cross_z()
    out.take(0)
    j4.ring.take(2)
    j4.cross_z()
    j1.middle()
    out.take(1)
    j2.begin()
    j1.end()
    j2.middle()

    for copy in gin_z:
        copy.wait_recv()

    def total(buf, got, cols):
        t = buf[y, zl, :, cols].astype(F32) + got[0, :, cols].astype(F32)
        return t + got[1, :, cols].astype(F32) + got[2, :, cols].astype(F32)

    dots = jnp.zeros((R, 128), F32)
    for i in range(D // 128):
        cols = slice(i * 128, (i + 1) * 128)
        g = total(px, zx, cols)
        t = x_ref[:, cols].astype(F32)
        gfull[:, cols] = g
        dots = dots + g * gain_ref[i : i + 1, :] * t
        gy[y, i : i + 1, :] = jnp.sum(g * t * inverse, axis=0, keepdims=True)
    gyx = [go(gy.at[y], gy.at[y], peer) for peer in y_peers]
    out.take(2)
    out_z = scatter_z(po, zo)
    mean = jnp.sum(dots, axis=1, keepdims=True) * (1.0 / D)
    cubed = inverse * inverse * inverse * mean
    for i in range(D // 128):
        cols = slice(i * 128, (i + 1) * 128)
        t = x_ref[:, cols].astype(F32)
        gin_ref[:, cols] = (
            inverse * (gfull[:, cols] * gain_ref[i : i + 1, :]) - t * cubed
        ).astype(BF16)

    for copy in gyx:
        copy.wait_recv()
    gzl[zl] = gy[0] + gy[1] + gy[2] + gy[3]
    gzx2 = [go(gzl.at[zl], gzl.at[zl], peer) for peer in z_peers]
    j2.end()
    j3.begin()

    for copy in gzx2:
        copy.wait_recv()
    gx[x] = gzl[0] + gzl[1] + gzl[2] + gzl[3]
    gxx = [go(gx.at[x], gx.at[x], peer) for peer in x_peers]
    j3.middle()
    j4.begin()

    for copy in gxx:
        copy.wait_recv()
    gc[c] = gx[0] + gx[1] + gx[2] + gx[3]
    gcx = go(gc.at[c], gc.at[c], other)
    j3.end()
    j4.middle()
    gcx.wait_recv()
    gh[zh] = gc[0] + gc[1]
    ghx = go(gh.at[zh], gh.at[zh], zfar)

    for copy in out_z:
        copy.wait_recv()
    for i in range(D // 128):
        cols = slice(i * 128, (i + 1) * 128)
        out_ref[:, cols] = total(po, zo, cols).astype(BF16)

    j4.end()
    ghx.wait_recv()
    gg_ref[...] = gh[0] + gh[1]
    for part in (j1, j2, j3, j4):
        part.finish()
    for copy in copies.all:
        copy.wait_send()
    assert len(copies.all) <= N_SEM, len(copies.all)


def per_device(inputs, norm_gain, w_up, w_down, grad_out):
    vmem = pl.BlockSpec(memory_space=pltpu.VMEM)
    hbm = pl.BlockSpec(memory_space=pl.ANY)
    scratch = [
        ((D, F), BF16), ((F, D), BF16),
        ((16, R, D), BF16), ((16, R, D), BF16),
        ((T, D), BF16), ((T, D), BF16),
        ((H, 2 * T), BF16), ((H, T), BF16), ((2 * T, H), BF16),
        ((T, F), F32), ((T, F), F32),
        ((2 * T, F), BF16), ((T, F), BF16), ((F, 2 * T), BF16),
        ((4, 4, R, D), BF16), ((4, 4, R, D), BF16),
        ((2, 3, 4, R, H), BF16), ((2, 3, 4, R, H), BF16),
        ((3, R, D), BF16), ((3, R, D), BF16),
        ((4, 4, 2, 80, F), BF16), ((4, 2, 3, 80, F), BF16), ((4, 2, 80, F), BF16),
        ((4, 8, 128), F32), ((4, 8, 128), F32),
        ((4, 20, 128), F32), ((4, 20, 128), F32), ((4, 20, 128), F32),
        ((2, 20, 128), F32), ((2, 20, 128), F32),
        ((R, D), F32),
    ]
    out, gin, gup, gdn, gg = pl.pallas_call(
        kernel,
        out_shape=(
            pltpu.VMEM((R, D), BF16),
            pltpu.VMEM((R, D), BF16),
            pltpu.VMEM((D, F), BF16),
            pltpu.VMEM((F, D), BF16),
            pltpu.VMEM((D // 128, 128), F32),
        ),
        in_specs=[vmem, vmem, hbm, hbm, vmem],
        out_specs=(vmem,) * 5,
        scratch_shapes=[pltpu.VMEM(s, t) for s, t in scratch]
        + [
            pltpu.SemaphoreType.DMA((N_SEM,)),
            pltpu.SemaphoreType.DMA((N_SEM,)),
            pltpu.SemaphoreType.DMA((2,)),
        ],
        compiler_params=pltpu.CompilerParams(
            collective_id=0, has_side_effects=True, vmem_limit_bytes=46 << 20
        ),
    )(inputs, norm_gain.reshape(D // 128, 128), w_up, w_down, grad_out)
    return out, gin, gup, gdn, gg.reshape(D)


def solution(mesh):
    return jax.shard_map(
        per_device,
        mesh=mesh,
        in_specs=(
            P(("dp", "tensor"), None),
            P(),
            P(None, "tensor"),
            P("tensor", None),
            P(("dp", "tensor"), None),
        ),
        out_specs=(
            P(("dp", "tensor"), None),
            P(("dp", "tensor"), None),
            P(None, "tensor"),
            P("tensor", None),
            P(),
        ),
        check_vma=False,
    )
```

```python
import functools

import jax
import jax.numpy as jnp
from jax import lax
from jax.experimental import pallas as pl
from jax.experimental.pallas import tpu as pltpu
from jax.sharding import PartitionSpec as P

MESH = pl.DeviceIdType.MESH
F32 = jnp.float32
BF16 = jnp.bfloat16

D = 2560
F = 640
T = 384
R = 24
H = D // 2
N_SEND, N_RECV = 94, 143

SINE = (
    0.9999999958410793,
    -6.579735564529717,
    12.987846451008128,
    -12.207473944175224,
    6.687349899038311,
    -2.367236060103434,
    0.5102235956366108,
)
NT = (((1,), (1,)), ((), ()))
NN = (((1,), (0,)), ((), ()))


def dot(a, b, dims=NN):
    return lax.dot_general(a, b, dims, preferred_element_type=F32)


def staircase(values):
    r = values - jnp.floor(values + 0.5)
    s = r * r
    p = jnp.full_like(s, SINE[-1])
    for c in SINE[-2::-1]:
        p = p * s + c
    return values - p * r


def block_peak(values):
    lane = lax.broadcasted_iota(jnp.int32, values.shape, 1)
    for s in (1, 2, 4, 8):
        up = pltpu.roll(values, s, 1)
        down = pltpu.roll(values, 128 - s, 1)
        values = jnp.maximum(values, jnp.where((lane & s) != 0, up, down))
    return values


def quantize(values, magnitude, floor):
    peak = jnp.maximum(block_peak(magnitude), floor)
    return peak * (1.0 / 6.0) * staircase(values * (6.0 / peak))


class Copies:
    def __init__(self, send, recv):
        self.send, self.recv = send, recv
        self.count, self.spare, self.most, self.open = 0, [], 0, []

    def start(self, src, dst, device):
        if self.spare:
            n = self.spare.pop()
        else:
            n = self.most
            self.most += 1
        copy = pltpu.make_async_remote_copy(
            src_ref=src,
            dst_ref=dst,
            send_sem=self.send.at[n],
            recv_sem=self.recv.at[self.count],
            device_id=device,
            device_id_type=MESH,
        )
        copy.start()
        self.count += 1
        self.open.append((copy, n))
        return copy

    def sent(self, upto=None):
        done = self.open[:upto]
        for copy, n in done:
            copy.wait_send()
            self.spare.append(n)
        self.open = self.open[len(done) :]


def kernel(
    x_hbm, gain_hbm, wu_hbm, wd_hbm, go_hbm,
    out_ref, gin_ref, gup_ref, gdn_ref, gg_ref,
    x_ref, gain_ref, wu, wd, cg, qg, c2, aa, ss, cc, ghq, pa, gz2, hq, ht,
    po, px, ro, rx, zo, zx, w, wr, wz,
    py, pz, gy, gzl, gx, gc, gh, gfull, mx, send, recv, local,
):
    dp, tn = lax.axis_index("dp"), lax.axis_index("tensor")
    zh, x, c = dp // 8, (dp // 2) % 4, dp % 2
    zl, y = tn // 4, tn % 4

    def dev(zh=zh, x=x, c=c, zl=zl, y=y):
        return ((zh * 4 + x) * 2 + c, zl * 4 + y)

    def mod(v):
        return lax.rem(v + 8, 4)

    def place(rel):
        return (rel + 1) % 4

    def block(rel, zz):
        return place(rel) * 4 + zz

    yp, ym = dev(y=mod(y + 1)), dev(y=mod(y - 1))
    xp, xm = dev(x=mod(x + 1)), dev(x=mod(x - 1))
    other = dev(c=1 - c)
    zfar = dev(zh=1 - zh)
    y_peers = [dev(y=mod(y + k)) for k in (1, 2, 3)]
    z_peers = [dev(zl=mod(zl + k)) for k in (1, 2, 3)]
    x_peers = [dev(x=mod(x + k)) for k in (1, 2, 3)]
    copies = Copies(send, recv)
    go = copies.start

    def load(src, dst, n):
        copy = pltpu.make_async_copy(src, dst, local.at[n])
        copy.start()
        return copy

    load_x = load(x_hbm, x_ref, 2)
    load_gain = load(gain_hbm, gain_ref, 3)
    load_own = load(go_hbm, cg.at[block(0, zl)], 4)
    load_up = load(wu_hbm, wu, 0)
    load_down = load(wd_hbm, wd, 1)

    barrier = pltpu.get_barrier_semaphore()
    peers = y_peers + z_peers + x_peers + [other, zfar]
    for peer in peers:
        pl.semaphore_signal(barrier, inc=1, device_id=peer, device_id_type=MESH)
    load_x.wait()
    wide = x_ref[...].astype(F32)
    inverse = lax.rsqrt(jnp.mean(wide * wide, axis=1, keepdims=True) + 1e-05)
    load_gain.wait()
    pl.semaphore_wait(barrier, len(peers))

    def gather_z(buf, src, k):
        return go(src, buf.at[block(0, zl)], z_peers[k - 1])

    def gather_y(buf, k, src=None):
        zz = mod(zl - k)
        src = buf.at[block(0, zz)] if src is None else src
        return go(src, buf.at[block(-1, zz)], yp), go(src, buf.at[block(1, zz)], ym)

    def forward(buf, k, pair):
        plus, minus = pair
        zz = mod(zl - k)
        left, right = (slice(None), pl.ds(0, H)), (slice(None), pl.ds(H, H))
        plus.wait_recv()
        a = go(buf.at[(block(-1, zz), *left)], buf.at[(block(2, zz), *left)], yp)
        minus.wait_recv()
        b = go(buf.at[(block(1, zz), *right)], buf.at[(block(2, zz), *right)], ym)
        return a, b

    cy, qy, cz, qz, cf, qf = {}, {}, {}, {}, [], []
    cy[0] = gather_y(cg, 0, go_hbm)
    cz[1] = gather_z(cg, go_hbm, 1)

    for i in range(D // 128):
        cols = slice(i * 128, (i + 1) * 128)
        normed = wide[:, cols] * inverse * gain_ref[i : i + 1, :]
        q = quantize(normed, jnp.abs(normed), 1.5)
        qg[block(0, zl), :, cols] = q.astype(BF16)

    mine = qg.at[block(0, zl)]
    qy[0] = gather_y(qg, 0)
    qz[1] = gather_z(qg, mine, 1)
    qz[3] = gather_z(qg, mine, 3)

    def next_q(k):
        qz[k].wait_recv()
        qy[k] = gather_y(qg, k)

    def next_c(k):
        cz[k].wait_recv()
        cy[k] = gather_y(cg, k)

    def forward_q(k):
        qf.extend(forward(qg, k, qy[k]))

    def forward_c(k):
        cf.extend(forward(cg, k, cy[k]))

    next_c(1)
    forward_c(0)
    forward_q(0)
    next_q(1)
    qz[2] = gather_z(qg, mine, 2)
    next_q(3)
    cz[3] = gather_z(cg, go_hbm, 3)
    forward_q(1)
    next_q(2)
    cz[2] = gather_z(cg, go_hbm, 2)
    forward_q(3)
    forward_c(1)
    next_c(3)
    forward_q(2)
    next_c(2)

    load_up.wait()
    near, last = (0, 12), (12, 4)

    def pre_group(group, most):
        b, n = group
        rows = slice(b * R, (b + n) * R)

        @pl.loop(0, 5)
        def _(i):
            ks = pl.ds(pl.multiple_of(i * 512, 512), 512)
            v = qg[b : b + n, :, ks].astype(F32).reshape(n * R, 512).astype(BF16)
            part = dot(v, wu[ks, :])

            @pl.when(i == 0)
            def _():
                pa[rows, :] = part

            @pl.when(i > 0)
            def _():
                pa[rows, :] += part

        @pl.loop(0, n)
        def _(i):
            at = pl.ds(pl.multiple_of(b * R + i * R, R), R)
            top = jnp.zeros((R, 128), F32)
            for j in range(F // 128):
                cols = slice(j * 128, (j + 1) * 128)
                active = jnp.maximum(pa[at, cols], 0.0)
                pa[at, cols] = active
                top = jnp.maximum(top, active)
            most[...] = jnp.maximum(most[...], top)

    mx[...] = jnp.zeros((R, 128), F32)
    pre_group(near, mx)
    for copy in qf:
        copy.wait_recv()
    forward_c(3)
    pre_group(last, mx)
    most = jnp.max(jnp.max(mx[...], axis=0, keepdims=True), axis=1, keepdims=True)
    py[y] = jnp.broadcast_to(most * most, (8, 128))
    pyx = [go(py.at[y], py.at[y], peer) for peer in y_peers]
    forward_c(2)

    def lay(i, start, put):
        cols = pl.ds(pl.multiple_of(start + i * 256, 256), 256)
        v = qg[:, :, cols].astype(F32).reshape(T, 256)
        put(pl.ds(pl.multiple_of(i * 256, 256), 256), v.T.astype(BF16))

    def put_other(rows, v):
        ss[rows, :] = v

    def put_own(rows, v):
        aa[rows, pl.ds(0, T)] = v

    @pl.loop(0, 5)
    def _(i):
        lay(i, (1 - c) * H, put_other)

    aax = go(ss, aa.at[:, pl.ds(T, T)], other)

    load_down.wait()
    other_half = pl.ds(pl.multiple_of((1 - c) * H, H), H)
    own_half = pl.ds(pl.multiple_of(c * H, H), H)
    gzx, ccx = [], []

    def grad_group(group):
        b, n = group
        rows = slice(b * R, (b + n) * R)

        @pl.loop(0, 5)
        def _(i):
            ks = pl.ds(pl.multiple_of(i * 512, 512), 512)
            v = cg[b : b + n, :, ks].astype(F32).reshape(n * R, 512).astype(BF16)
            c2[rows, ks] = v
            part = dot(v, wd[:, ks], NT)

            @pl.when(i == 0)
            def _():
                ghq[rows, :] = part

            @pl.when(i > 0)
            def _():
                ghq[rows, :] += part

        @pl.loop(0, n // 2)
        def _(i):
            at = pl.ds(pl.multiple_of(b * R + i * 2 * R, 2 * R), 2 * R)
            for j in range(F // 128):
                cols = slice(j * 128, (j + 1) * 128)
                gz2[at, cols] = (ghq[at, cols] * 2.0 * pa[at, cols]).astype(BF16)

        far = slice(T + b * R, T + (b + n) * R)
        gzx.append(go(gz2.at[rows], gz2.at[far], other))
        ccx.append(go(c2.at[rows, other_half], cc.at[far], other))

    load_own.wait()
    grad_group(near)

    @pl.loop(0, 5)
    def _(i):
        lay(i, c * H, put_own)

    for copy in pyx:
        copy.wait_recv()
    peak = jnp.maximum(jnp.maximum(py[0], py[1]), jnp.maximum(py[2], py[3]))
    pz[zl] = peak
    pzx = [go(pz.at[zl], pz.at[zl], peer) for peer in z_peers]
    for copy in cf:
        copy.wait_recv()
    grad_group(last)

    class Ring:
        def __init__(self, plus, minus, view, got, tiles, cut):
            self.to = (plus, minus)
            self.view, self.got, self.tiles, self.cut = view, got, tiles, cut
            self.last = [None, None]

        def send(self, s, way):
            at = self.view(-1 - s if way == 0 else 1 + s, way)
            self.last[way] = go(at, self.got.at[way, s], self.to[way])

        def take(self, s):
            for way in (0, 1):
                self.last[way].wait_recv()
                mine = self.view(-2 - s if way == 0 else 2 + s, way)
                theirs = self.got.at[way, s]

                @pl.loop(0, self.tiles)
                def _(i):
                    at = self.cut(i)
                    both = mine[at].astype(F32) + theirs[at].astype(F32)
                    mine[at] = both.astype(BF16)

                if s < 2:
                    self.send(s + 1, way)

    class Part:
        def __init__(self, n, buf, where):
            self.n, self.buf, self.where = n, buf, where
            self.ring = Ring(
                xp, xm, lambda rel, way: w.at[n, mod(x + rel), way], wr.at[n], 5,
                lambda i: pl.ds(pl.multiple_of(i * 16, 16), 16),
            )

        def cross_z(self):
            self.far = go(w.at[self.n, x], wz.at[self.n], zfar)

        def begin(self):
            self.far.wait_recv()
            for way in (0, 1):
                both = w[self.n, x, way].astype(F32) + wz[self.n, way].astype(F32)
                self.buf[self.where(c, x, way)] = both.astype(BF16)
            at = self.buf.at[self.where(c, x)]
            self.plus, self.minus = go(at, at, xp), go(at, at, xm)
            self.cross = [go(at, at, other)]

        def middle(self):
            self.plus.wait_recv()
            at = self.buf.at[self.where(c, mod(x - 1), 0)]
            self.fplus = go(at, at, xp)
            at = self.buf.at[self.where(c, mod(x - 1))]
            self.cross.append(go(at, at, other))
            self.minus.wait_recv()
            at = self.buf.at[self.where(c, mod(x + 1), 1)]
            self.fminus = go(at, at, xm)
            at = self.buf.at[self.where(c, mod(x + 1))]
            self.cross.append(go(at, at, other))

        def end(self):
            self.fplus.wait_recv()
            at = self.buf.at[self.where(c, mod(x + 2), 0)]
            self.cross.append(go(at, at, other))
            self.fminus.wait_recv()
            at = self.buf.at[self.where(c, mod(x + 2), 1)]
            self.cross.append(go(at, at, other))

        def finish(self):
            for copy in self.cross:
                copy.wait_recv()

    def up_rows(p):
        def where(core, j, way=None):
            start = core * H + j * 320 + p * 160 + (0 if way is None else way * 80)
            n = 160 if way is None else 80
            return (pl.ds(pl.multiple_of(start, n), n), slice(None))

        return where

    def down_rows(p):
        def where(core, j, way=None):
            cols = pl.ds(pl.multiple_of(core * H + p * F, 128), F)
            start = j * 160 + (0 if way is None else way * 80)
            n = 160 if way is None else 80
            return (pl.ds(pl.multiple_of(start, n), n), cols)

        return where

    j1, j2 = Part(0, gup_ref, up_rows(0)), Part(1, gup_ref, up_rows(1))
    j3, j4 = Part(2, gdn_ref, down_rows(0)), Part(3, gdn_ref, down_rows(1))

    def p_view(buf):
        return lambda rel, way: buf.at[place(rel), :, :, pl.ds(way * H, H)]

    out = Ring(yp, ym, p_view(po), ro, 4, lambda i: i)
    gin = Ring(yp, ym, p_view(px), rx, 4, lambda i: i)

    aax.wait_recv()
    for copy in gzx:
        copy.wait_recv()

    def up_chunk(p, j):
        rows = pl.ds(pl.multiple_of(j * 320 + p * 160, 160), 160)
        w[p, j] = dot(aa[rows, :], gz2[...]).reshape(2, 80, F).astype(BF16)

    mark = len(copies.open)
    up_chunk(0, mod(x - 1))
    j1.ring.send(0, 0)
    up_chunk(0, mod(x + 1))
    j1.ring.send(0, 1)
    up_chunk(0, mod(x + 2))

    @pl.loop(0, 5)
    def _(i):
        ns = pl.ds(pl.multiple_of(i * 512, 512), 512)
        part = dot(gz2[pl.ds(0, T), :], wu[ns, :], NT)
        px[:, :, :, ns] = part.reshape(4, 4, R, 512).astype(BF16)

    gin.send(0, 0)
    gin.send(0, 1)
    j1.ring.take(0)
    up_chunk(0, x)
    copies.sent(mark)

    for copy in pzx:
        copy.wait_recv()
    peak = jnp.maximum(jnp.maximum(pz[0], pz[1]), jnp.maximum(pz[2], pz[3]))
    floor = ((peak[0:1, :] + 1e-06) * 0.125).reshape(1, 1, 128)

    def hidden_tile(i):
        rows = slice(i * 128, (i + 1) * 128)

        @pl.loop(0, F // 128)
        def _(j):
            cols = pl.ds(pl.multiple_of(j * 128, 128), 128)
            active = pa[rows, cols]
            hidden = (active * active).T.reshape(8, 16, 128)
            most = jnp.maximum(jnp.max(hidden, axis=1, keepdims=True), floor)
            q = most * (1.0 / 6.0) * staircase(hidden * (6.0 / most))
            q = q.reshape(128, 128)
            ht[cols, rows] = q.astype(BF16)
            hq[rows, cols] = q.T.astype(BF16)

    hidden_tile(0)
    up_chunk(1, mod(x - 1))
    up_chunk(1, mod(x + 1))
    j1.ring.take(1)
    j2.ring.send(0, 0)
    j2.ring.send(0, 1)
    hidden_tile(1)
    up_chunk(1, mod(x + 2))
    up_chunk(1, x)
    hidden_tile(2)
    htx = go(ht.at[:, pl.ds(0, T)], ht.at[:, pl.ds(T, T)], other)
    gin.take(0)

    def down_chunk(j):
        rows = pl.ds(pl.multiple_of(j * 160, 160), 160)
        for p in (0, 1):
            part = dot(ht[rows, :], cc[:, p * F : (p + 1) * F])
            w[2 + p, j] = part.reshape(2, 80, F).astype(BF16)

    j1.ring.take(2)
    j1.cross_z()
    j2.ring.take(0)
    cc[pl.ds(0, T), :] = c2[:, own_half]
    for copy in ccx:
        copy.wait_recv()
    htx.wait_recv()
    down_chunk(mod(x - 1))
    j3.ring.send(0, 0)
    down_chunk(mod(x + 1))
    j3.ring.send(0, 1)
    j2.ring.take(1)
    gin.take(1)
    down_chunk(mod(x + 2))
    down_chunk(x)

    def out_tile(i):
        ns = slice(i * 512, (i + 1) * 512)
        part = dot(hq[...], wd[:, ns])
        po[:, :, :, ns] = part.reshape(4, 4, R, 512).astype(BF16)

    out_tile(0)
    j2.ring.take(2)
    j2.cross_z()
    j4.ring.send(0, 0)
    j4.ring.send(0, 1)
    out_tile(1)
    j3.ring.take(0)
    out_tile(2)
    out_tile(3)
    out_tile(4)
    out.send(0, 0)
    out.send(0, 1)

    def scatter_z(buf, got):
        return [
            go(buf.at[place(0), mod(zl + k)], got.at[k - 1], z_peers[k - 1]) for k in (1, 2, 3)
        ]

    gin.take(2)
    gin_z = scatter_z(px, zx)
    j3.ring.take(1)
    j4.ring.take(0)
    j1.begin()
    j3.ring.take(2)
    j3.cross_z()
    j4.ring.take(1)
    out.take(0)
    j4.ring.take(2)
    j4.cross_z()
    j1.middle()
    j2.begin()
    out.take(1)
    j1.end()
    j2.middle()
    out.take(2)
    out_z = scatter_z(po, zo)
    j2.end()

    for copy in gin_z:
        copy.wait_recv()

    def total(buf, got, cols):
        t = buf[place(0), zl, :, cols].astype(F32) + got[0, :, cols].astype(F32)
        return t + got[1, :, cols].astype(F32) + got[2, :, cols].astype(F32)

    dots = jnp.zeros((R, 128), F32)
    for i in range(D // 128):
        cols = slice(i * 128, (i + 1) * 128)
        g = total(px, zx, cols)
        t = x_ref[:, cols].astype(F32)
        gfull[:, cols] = g
        dots = dots + g * gain_ref[i : i + 1, :] * t
        gy[y, i : i + 1, :] = jnp.sum(g * t * inverse, axis=0, keepdims=True)
    gyx = [go(gy.at[y], gy.at[y], peer) for peer in y_peers]
    j3.begin()
    mean = jnp.sum(dots, axis=1, keepdims=True) * (1.0 / D)
    cubed = inverse * inverse * inverse * mean
    for i in range(D // 128):
        cols = slice(i * 128, (i + 1) * 128)
        t = x_ref[:, cols].astype(F32)
        gin_ref[:, cols] = (
            inverse * (gfull[:, cols] * gain_ref[i : i + 1, :]) - t * cubed
        ).astype(BF16)

    for copy in gyx:
        copy.wait_recv()
    gzl[zl] = gy[0] + gy[1] + gy[2] + gy[3]
    gzx2 = [go(gzl.at[zl], gzl.at[zl], peer) for peer in z_peers]
    j3.middle()
    j4.begin()
    for copy in gzx2:
        copy.wait_recv()
    gx[x] = gzl[0] + gzl[1] + gzl[2] + gzl[3]
    gxx = [go(gx.at[x], gx.at[x], peer) for peer in x_peers]
    j3.end()
    for copy in gxx:
        copy.wait_recv()
    gc[c] = gx[0] + gx[1] + gx[2] + gx[3]
    gcx = go(gc.at[c], gc.at[c], other)
    j4.middle()
    gcx.wait_recv()
    gh[zh] = gc[0] + gc[1]
    ghx = go(gh.at[zh], gh.at[zh], zfar)

    for copy in out_z:
        copy.wait_recv()
    for i in range(D // 128):
        cols = slice(i * 128, (i + 1) * 128)
        out_ref[:, cols] = total(po, zo, cols).astype(BF16)

    j4.end()
    ghx.wait_recv()
    gg_ref[...] = gh[0] + gh[1]
    for part in (j1, j2, j3, j4):
        part.finish()
    copies.sent()
    assert (copies.most, copies.count) == (N_SEND, N_RECV), (copies.most, copies.count)


def per_device(inputs, norm_gain, w_up, w_down, grad_out):
    vmem = pl.BlockSpec(memory_space=pltpu.VMEM)
    hbm = pl.BlockSpec(memory_space=pltpu.HBM)
    scratch = [
        ((R, D), BF16), ((D // 128, 128), F32),
        ((D, F), BF16), ((F, D), BF16),
        ((16, R, D), BF16), ((16, R, D), BF16),
        ((T, D), BF16),
        ((H, 2 * T), BF16), ((H, T), BF16), ((2 * T, H), BF16),
        ((T, F), F32), ((T, F), F32),
        ((2 * T, F), BF16), ((T, F), BF16), ((F, 2 * T), BF16),
        ((4, 4, R, D), BF16), ((4, 4, R, D), BF16),
        ((2, 3, 4, R, H), BF16), ((2, 3, 4, R, H), BF16),
        ((3, R, D), BF16), ((3, R, D), BF16),
        ((4, 4, 2, 80, F), BF16), ((4, 2, 3, 80, F), BF16), ((4, 2, 80, F), BF16),
        ((4, 8, 128), F32), ((4, 8, 128), F32),
        ((4, 20, 128), F32), ((4, 20, 128), F32), ((4, 20, 128), F32),
        ((2, 20, 128), F32), ((2, 20, 128), F32),
        ((R, D), F32), ((R, 128), F32),
    ]
    out, gin, gup, gdn, gg = pl.pallas_call(
        kernel,
        out_shape=(
            pltpu.VMEM((R, D), BF16),
            pltpu.VMEM((R, D), BF16),
            pltpu.VMEM((D, F), BF16),
            pltpu.VMEM((F, D), BF16),
            pltpu.VMEM((D // 128, 128), F32),
        ),
        in_specs=[hbm] * 5,
        out_specs=(vmem,) * 5,
        scratch_shapes=[pltpu.VMEM(s, t) for s, t in scratch]
        + [
            pltpu.SemaphoreType.DMA((N_SEND,)),
            pltpu.SemaphoreType.DMA((N_RECV,)),
            pltpu.SemaphoreType.DMA((5,)),
        ],
        compiler_params=pltpu.CompilerParams(
            collective_id=0, has_side_effects=True, vmem_limit_bytes=46 << 20
        ),
    )(inputs, norm_gain.reshape(D // 128, 128), w_up, w_down, grad_out)
    return out, gin, gup, gdn, gg.reshape(D)


def solution(mesh):
    return jax.shard_map(
        per_device,
        mesh=mesh,
        in_specs=(
            P(("dp", "tensor"), None),
            P(),
            P(None, "tensor"),
            P("tensor", None),
            P(("dp", "tensor"), None),
        ),
        out_specs=(
            P(("dp", "tensor"), None),
            P(("dp", "tensor"), None),
            P(None, "tensor"),
            P("tensor", None),
            P(),
        ),
        check_vma=False,
    )
```

```python
import functools

import jax
import jax.numpy as jnp
from jax import lax
from jax.experimental import pallas as pl
from jax.experimental.pallas import tpu as pltpu
from jax.sharding import PartitionSpec as P

MESH = pl.DeviceIdType.MESH
F32 = jnp.float32
BF16 = jnp.bfloat16

D = 2560
F = 640
T = 384
R = 24
H = D // 2
N_SEND, N_RECV = 95, 150

SINE = (
    0.9999999958410793,
    -6.579735564529717,
    12.987846451008128,
    -12.207473944175224,
    6.687349899038311,
    -2.367236060103434,
    0.5102235956366108,
)
NT = (((1,), (1,)), ((), ()))
NN = (((1,), (0,)), ((), ()))


def dot(a, b, dims=NN):
    return lax.dot_general(a, b, dims, preferred_element_type=F32)


def staircase(values):
    r = values - jnp.floor(values + 0.5)
    s = r * r
    p = jnp.full_like(s, SINE[-1])
    for c in SINE[-2::-1]:
        p = p * s + c
    return values - p * r


def block_peak(values):
    lane = lax.broadcasted_iota(jnp.int32, values.shape, 1)
    for s in (1, 2, 4, 8):
        up = pltpu.roll(values, s, 1)
        down = pltpu.roll(values, 128 - s, 1)
        values = jnp.maximum(values, jnp.where((lane & s) != 0, up, down))
    return values


def quantize(values, magnitude, floor):
    peak = jnp.maximum(block_peak(magnitude), floor)
    return peak * (1.0 / 6.0) * staircase(values * (6.0 / peak))


class Copies:
    def __init__(self, send, recv):
        self.send, self.recv = send, recv
        self.count, self.spare, self.most, self.open = 0, [], 0, []

    def start(self, src, dst, device):
        if self.spare:
            n = self.spare.pop()
        else:
            n = self.most
            self.most += 1
        copy = pltpu.make_async_remote_copy(
            src_ref=src,
            dst_ref=dst,
            send_sem=self.send.at[n],
            recv_sem=self.recv.at[self.count],
            device_id=device,
            device_id_type=MESH,
        )
        copy.start()
        self.count += 1
        self.open.append((copy, n))
        return copy

    def sent(self, upto=None):
        done = self.open[:upto]
        for copy, n in done:
            copy.wait_send()
            self.spare.append(n)
        self.open = self.open[len(done) :]


def kernel(
    x_hbm, gain_hbm, wu_hbm, wd_hbm, go_hbm,
    out_ref, gin_ref, gup_ref, gdn_ref, gg_ref,
    x_ref, gain_ref, wu, wd, cg, qg, c2, aa, ss, cc, ghq, pa, gz2, hq, ht,
    po, px, ro, rx, zo, zx, w, wr, wz,
    py, pz, gy, gzl, gx, gc, gh, xg, ig, gfull, mx, send, recv, local,
):
    dp, tn = lax.axis_index("dp"), lax.axis_index("tensor")
    zh, x, c = dp // 8, (dp // 2) % 4, dp % 2
    zl, y = tn // 4, tn % 4

    def dev(zh=zh, x=x, c=c, zl=zl, y=y):
        return ((zh * 4 + x) * 2 + c, zl * 4 + y)

    def mod(v):
        return lax.rem(v + 8, 4)

    def place(rel):
        return (rel + 1) % 4

    def block(rel, zz):
        return place(rel) * 4 + zz

    yp, ym = dev(y=mod(y + 1)), dev(y=mod(y - 1))
    xp, xm = dev(x=mod(x + 1)), dev(x=mod(x - 1))
    other = dev(c=1 - c)
    zfar = dev(zh=1 - zh)
    y_peers = [dev(y=mod(y + k)) for k in (1, 2, 3)]
    z_peers = [dev(zl=mod(zl + k)) for k in (1, 2, 3)]
    x_peers = [dev(x=mod(x + k)) for k in (1, 2, 3)]
    copies = Copies(send, recv)
    go = copies.start

    def load(src, dst, n):
        copy = pltpu.make_async_copy(src, dst, local.at[n])
        copy.start()
        return copy

    load_x = load(x_hbm, x_ref, 2)
    load_gain = load(gain_hbm, gain_ref, 3)
    load_own = load(go_hbm, cg.at[block(0, zl)], 4)
    load_up = load(wu_hbm, wu, 0)
    load_down = load(wd_hbm, wd, 1)

    barrier = pltpu.get_barrier_semaphore()
    peers = y_peers + z_peers + x_peers + [other, zfar]
    for peer in peers:
        pl.semaphore_signal(barrier, inc=1, device_id=peer, device_id_type=MESH)
    load_x.wait()
    wide = x_ref[...].astype(F32)
    inverse = lax.rsqrt(jnp.mean(wide * wide, axis=1, keepdims=True) + 1e-05)
    ig[zl] = jnp.broadcast_to(inverse, (R, 128))
    xg[zl] = x_ref[...]
    load_gain.wait()
    pl.semaphore_wait(barrier, len(peers))

    def gather_z(buf, src, k):
        return go(src, buf.at[block(0, zl)], z_peers[k - 1])

    def gather_y(buf, k, src=None):
        zz = mod(zl - k)
        src = buf.at[block(0, zz)] if src is None else src
        return go(src, buf.at[block(-1, zz)], yp), go(src, buf.at[block(1, zz)], ym)

    def forward(buf, k, pair):
        plus, minus = pair
        zz = mod(zl - k)
        left, right = (slice(None), pl.ds(0, H)), (slice(None), pl.ds(H, H))
        plus.wait_recv()
        a = go(buf.at[(block(-1, zz), *left)], buf.at[(block(2, zz), *left)], yp)
        minus.wait_recv()
        b = go(buf.at[(block(1, zz), *right)], buf.at[(block(2, zz), *right)], ym)
        return a, b

    cy, qy, cz, qz, cf, qf = {}, {}, {}, {}, [], []
    cy[0] = gather_y(cg, 0, go_hbm)
    cz[1] = gather_z(cg, go_hbm, 1)

    for i in range(D // 128):
        cols = slice(i * 128, (i + 1) * 128)
        normed = wide[:, cols] * inverse * gain_ref[i : i + 1, :]
        q = quantize(normed, jnp.abs(normed), 1.5)
        qg[block(0, zl), :, cols] = q.astype(BF16)

    mine = qg.at[block(0, zl)]
    qy[0] = gather_y(qg, 0)
    qz[1] = gather_z(qg, mine, 1)
    qz[3] = gather_z(qg, mine, 3)

    def next_q(k):
        qz[k].wait_recv()
        qy[k] = gather_y(qg, k)

    def next_c(k):
        cz[k].wait_recv()
        cy[k] = gather_y(cg, k)

    def forward_q(k):
        qf.extend(forward(qg, k, qy[k]))

    def forward_c(k):
        cf.extend(forward(cg, k, cy[k]))

    next_c(1)
    forward_c(0)
    forward_q(0)
    next_q(1)
    qz[2] = gather_z(qg, mine, 2)
    next_q(3)
    cz[3] = gather_z(cg, go_hbm, 3)
    forward_q(1)
    next_q(2)
    cz[2] = gather_z(cg, go_hbm, 2)
    forward_q(3)
    forward_c(1)
    next_c(3)
    forward_q(2)
    next_c(2)
    xz = [go(x_ref, xg.at[zl], peer) for peer in z_peers]
    xz += [go(ig.at[zl], ig.at[zl], peer) for peer in z_peers]

    load_up.wait()
    near, last = (0, 12), (12, 4)

    def pre_group(group, most):
        b, n = group
        rows = slice(b * R, (b + n) * R)

        @pl.loop(0, 5)
        def _(i):
            ks = pl.ds(pl.multiple_of(i * 512, 512), 512)
            v = qg[b : b + n, :, ks].astype(F32).reshape(n * R, 512).astype(BF16)
            part = dot(v, wu[ks, :])

            @pl.when(i == 0)
            def _():
                pa[rows, :] = part

            @pl.when(i > 0)
            def _():
                pa[rows, :] += part

        @pl.loop(0, n)
        def _(i):
            at = pl.ds(pl.multiple_of(b * R + i * R, R), R)
            top = jnp.zeros((R, 128), F32)
            for j in range(F // 128):
                cols = slice(j * 128, (j + 1) * 128)
                active = jnp.maximum(pa[at, cols], 0.0)
                pa[at, cols] = active
                top = jnp.maximum(top, active)
            most[...] = jnp.maximum(most[...], top)

    mx[...] = jnp.zeros((R, 128), F32)
    pre_group(near, mx)
    for copy in qf:
        copy.wait_recv()
    forward_c(3)
    pre_group(last, mx)
    most = jnp.max(jnp.max(mx[...], axis=0, keepdims=True), axis=1, keepdims=True)
    py[y] = jnp.broadcast_to(most * most, (8, 128))
    pyx = [go(py.at[y], py.at[y], peer) for peer in y_peers]
    forward_c(2)

    def lay(i, start, put):
        cols = pl.ds(pl.multiple_of(start + i * 256, 256), 256)
        v = qg[:, :, cols].astype(F32).reshape(T, 256)
        put(pl.ds(pl.multiple_of(i * 256, 256), 256), v.T.astype(BF16))

    def put_other(rows, v):
        ss[rows, :] = v

    def put_own(rows, v):
        aa[rows, pl.ds(0, T)] = v

    @pl.loop(0, 5)
    def _(i):
        lay(i, (1 - c) * H, put_other)

    aax = go(ss, aa.at[:, pl.ds(T, T)], other)

    load_down.wait()
    other_half = pl.ds(pl.multiple_of((1 - c) * H, H), H)
    own_half = pl.ds(pl.multiple_of(c * H, H), H)
    gzx, ccx = [], []

    def grad_group(group):
        b, n = group
        rows = slice(b * R, (b + n) * R)

        @pl.loop(0, 5)
        def _(i):
            ks = pl.ds(pl.multiple_of(i * 512, 512), 512)
            v = cg[b : b + n, :, ks].astype(F32).reshape(n * R, 512).astype(BF16)
            c2[rows, ks] = v
            part = dot(v, wd[:, ks], NT)

            @pl.when(i == 0)
            def _():
                ghq[rows, :] = part

            @pl.when(i > 0)
            def _():
                ghq[rows, :] += part

        @pl.loop(0, n // 2)
        def _(i):
            at = pl.ds(pl.multiple_of(b * R + i * 2 * R, 2 * R), 2 * R)
            for j in range(F // 128):
                cols = slice(j * 128, (j + 1) * 128)
                gz2[at, cols] = (ghq[at, cols] * 2.0 * pa[at, cols]).astype(BF16)

        far = slice(T + b * R, T + (b + n) * R)
        gzx.append(go(gz2.at[rows], gz2.at[far], other))
        ccx.append(go(c2.at[rows, other_half], cc.at[far], other))

    load_own.wait()
    grad_group(near)

    for copy in pyx:
        copy.wait_recv()
    peak = jnp.maximum(jnp.maximum(py[0], py[1]), jnp.maximum(py[2], py[3]))
    pz[zl] = peak
    pzx = [go(pz.at[zl], pz.at[zl], peer) for peer in z_peers]
    for copy in cf:
        copy.wait_recv()
    grad_group(last)

    @pl.loop(0, 5)
    def _(i):
        lay(i, c * H, put_own)


    class Ring:
        def __init__(self, plus, minus, view, got, tiles, cut):
            self.to = (plus, minus)
            self.view, self.got, self.tiles, self.cut = view, got, tiles, cut
            self.last = [None, None]

        def send(self, s, way):
            at = self.view(-1 - s if way == 0 else 1 + s, way)
            self.last[way] = go(at, self.got.at[way, s], self.to[way])

        def take(self, s):
            for way in (0, 1):
                self.last[way].wait_recv()
                mine = self.view(-2 - s if way == 0 else 2 + s, way)
                theirs = self.got.at[way, s]

                @pl.loop(0, self.tiles)
                def _(i):
                    at = self.cut(i)
                    both = mine[at].astype(F32) + theirs[at].astype(F32)
                    mine[at] = both.astype(BF16)

                if s < 2:
                    self.send(s + 1, way)

    class Part:
        def __init__(self, n, buf, where):
            self.n, self.buf, self.where = n, buf, where
            self.ring = Ring(
                xp, xm, lambda rel, way: w.at[n, mod(x + rel), way], wr.at[n], 5,
                lambda i: pl.ds(pl.multiple_of(i * 16, 16), 16),
            )

        def cross_z(self):
            self.far = [go(w.at[self.n, x], wz.at[self.n], zfar)]

        def begin(self):
            for copy in self.far:
                copy.wait_recv()
            for way in (0, 1):
                both = w[self.n, x, way].astype(F32) + wz[self.n, way].astype(F32)
                self.buf[self.where(c, x, way)] = both.astype(BF16)
            at = self.buf.at[self.where(c, x)]
            self.plus, self.minus = go(at, at, xp), go(at, at, xm)
            self.cross = [go(at, at, other)]

        def middle(self):
            self.plus.wait_recv()
            at = self.buf.at[self.where(c, mod(x - 1), 0)]
            self.fplus = go(at, at, xp)
            at = self.buf.at[self.where(c, mod(x - 1))]
            self.cross.append(go(at, at, other))
            self.minus.wait_recv()
            at = self.buf.at[self.where(c, mod(x + 1), 1)]
            self.fminus = go(at, at, xm)
            at = self.buf.at[self.where(c, mod(x + 1))]
            self.cross.append(go(at, at, other))

        def end(self):
            self.fplus.wait_recv()
            at = self.buf.at[self.where(c, mod(x + 2), 0)]
            self.cross.append(go(at, at, other))
            self.fminus.wait_recv()
            at = self.buf.at[self.where(c, mod(x + 2), 1)]
            self.cross.append(go(at, at, other))

        def finish(self):
            for copy in self.cross:
                copy.wait_recv()

    class First(Part):
        def __init__(self, *args):
            super().__init__(*args)
            self.got, self.far = [None, None], []

        def send(self, half):
            self.got[half] = [
                go(w.at[self.n, mod(x + k), half], wr.at[self.n, half, k - 1], x_peers[k - 1])
                for k in (1, 3, 2)
            ]

        def take(self, half):
            for copy in self.got[half]:
                copy.wait_recv()
            mine, got = w.at[self.n, x, half], wr.at[self.n, half]

            @pl.loop(0, 5)
            def _(i):
                at = pl.ds(pl.multiple_of(i * 16, 16), 16)
                t = mine[at].astype(F32) + got[0, at].astype(F32)
                t = t + got[1, at].astype(F32) + got[2, at].astype(F32)
                mine[at] = t.astype(BF16)

            self.far.append(go(mine, wz.at[self.n, half], zfar))

    def up_rows(p):
        def where(core, j, way=None):
            start = core * H + j * 320 + p * 160 + (0 if way is None else way * 80)
            n = 160 if way is None else 80
            return (pl.ds(pl.multiple_of(start, n), n), slice(None))

        return where

    def down_rows(p):
        def where(core, j, way=None):
            cols = pl.ds(pl.multiple_of(core * H + p * F, 128), F)
            start = j * 160 + (0 if way is None else way * 80)
            n = 160 if way is None else 80
            return (pl.ds(pl.multiple_of(start, n), n), cols)

        return where

    j1, j2 = First(0, gup_ref, up_rows(0)), Part(1, gup_ref, up_rows(1))
    j3, j4 = Part(2, gdn_ref, down_rows(0)), Part(3, gdn_ref, down_rows(1))

    def p_view(buf):
        return lambda rel, way: buf.at[place(rel), :, :, pl.ds(way * H, H)]

    out = Ring(yp, ym, p_view(po), ro, 4, lambda i: i)
    gin = Ring(yp, ym, p_view(px), rx, 4, lambda i: i)

    aax.wait_recv()
    for copy in gzx:
        copy.wait_recv()

    def up_chunk(p, j):
        rows = pl.ds(pl.multiple_of(j * 320 + p * 160, 160), 160)
        w[p, j] = dot(aa[rows, :], gz2[...]).reshape(2, 80, F).astype(BF16)

    mark = len(copies.open)
    def up_half(half):
        for k in (1, 3, 2, 0):
            j = mod(x + k)
            rows = pl.ds(pl.multiple_of(j * 320 + half * 80, 16), 80)
            w[0, j, half] = dot(aa[rows, :], gz2[...]).astype(BF16)

    up_half(0)
    j1.send(0)
    up_half(1)
    j1.send(1)

    @pl.loop(0, 5)
    def _(i):
        ns = pl.ds(pl.multiple_of(i * 512, 512), 512)
        part = dot(gz2[pl.ds(0, T), :], wu[ns, :], NT)
        px[:, :, :, ns] = part.reshape(4, 4, R, 512).astype(BF16)

    gin.send(0, 0)
    gin.send(0, 1)
    up_chunk(1, mod(x - 1))
    j2.ring.send(0, 0)
    up_chunk(1, mod(x + 1))
    j2.ring.send(0, 1)

    for copy in pzx:
        copy.wait_recv()
    peak = jnp.maximum(jnp.maximum(pz[0], pz[1]), jnp.maximum(pz[2], pz[3]))
    floor = ((peak[0:1, :] + 1e-06) * 0.125).reshape(1, 1, 128)

    def hidden_tile(i):
        rows = slice(i * 128, (i + 1) * 128)

        @pl.loop(0, F // 128)
        def _(j):
            cols = pl.ds(pl.multiple_of(j * 128, 128), 128)
            active = pa[rows, cols]
            hidden = (active * active).T.reshape(8, 16, 128)
            most = jnp.maximum(jnp.max(hidden, axis=1, keepdims=True), floor)
            q = most * (1.0 / 6.0) * staircase(hidden * (6.0 / most))
            q = q.reshape(128, 128)
            ht[cols, rows] = q.astype(BF16)
            hq[rows, cols] = q.T.astype(BF16)

    hidden_tile(0)
    hidden_tile(1)
    j1.take(0)
    hidden_tile(2)
    htx = go(ht.at[:, pl.ds(0, T)], ht.at[:, pl.ds(T, T)], other)

    def down_chunk(j):
        rows = pl.ds(pl.multiple_of(j * 160, 160), 160)
        for p in (0, 1):
            part = dot(ht[rows, :], cc[:, p * F : (p + 1) * F])
            w[2 + p, j] = part.reshape(2, 80, F).astype(BF16)

    up_chunk(1, mod(x + 2))
    cc[pl.ds(0, T), :] = c2[:, own_half]
    copies.sent(mark)
    for copy in ccx:
        copy.wait_recv()
    htx.wait_recv()
    down_chunk(mod(x - 1))
    j3.ring.send(0, 0)
    down_chunk(mod(x + 1))
    j3.ring.send(0, 1)
    j2.ring.take(0)
    j1.take(1)
    gin.take(0)
    j4.ring.send(0, 0)
    j4.ring.send(0, 1)
    up_chunk(1, x)
    down_chunk(mod(x + 2))
    down_chunk(x)

    def out_tile(i):
        ns = slice(i * 512, (i + 1) * 512)
        part = dot(hq[...], wd[:, ns])
        po[:, :, :, ns] = part.reshape(4, 4, R, 512).astype(BF16)

    out_tile(0)
    j2.ring.take(1)
    out_tile(1)
    j3.ring.take(0)
    out_tile(2)
    gin.take(1)
    out_tile(3)
    out_tile(4)
    out.send(0, 0)
    out.send(0, 1)

    def scatter_z(buf, got):
        return [
            go(buf.at[place(0), mod(zl + k)], got.at[k - 1], z_peers[k - 1]) for k in (1, 2, 3)
        ]

    j2.ring.take(2)
    j2.cross_z()
    j4.ring.take(0)
    j3.ring.take(1)
    gin.take(2)
    gin_z = scatter_z(px, zx)

    for copy in xz:
        copy.wait_recv()
    for i in range(D // 128):
        cols = slice(i * 128, (i + 1) * 128)
        t = jnp.zeros((R, 128), F32)
        for k in range(4):
            g = px[place(0), k, :, cols].astype(F32)
            t = t + g * xg[k, :, cols].astype(F32) * ig[k]
        gy[y, i : i + 1, :] = jnp.sum(t, axis=0, keepdims=True)
    gyx = [go(gy.at[y], gy.at[y], peer) for peer in y_peers]

    j1.begin()
    j4.ring.take(1)
    j3.ring.take(2)
    j3.cross_z()
    for copy in gyx:
        copy.wait_recv()
    gx[x] = gy[0] + gy[1] + gy[2] + gy[3]
    gxx = [go(gx.at[x], gx.at[x], peer) for peer in x_peers]
    out.take(0)
    j1.middle()
    j4.ring.take(2)
    j4.cross_z()
    j2.begin()
    j1.end()
    out.take(1)
    j2.middle()
    out.take(2)
    for copy in gxx:
        copy.wait_recv()
    gc[c] = gx[0] + gx[1] + gx[2] + gx[3]
    gcx = go(gc.at[c], gc.at[c], other)
    j2.end()
    gcx.wait_recv()
    gzl[zl] = gc[0] + gc[1]
    gzx2 = [go(gzl.at[zl], gzl.at[zl], peer) for peer in z_peers]
    j3.begin()
    j3.middle()
    j4.begin()
    for copy in gzx2:
        copy.wait_recv()
    gh[zh] = gzl[0] + gzl[1] + gzl[2] + gzl[3]
    ghx = go(gh.at[zh], gh.at[zh], zfar)
    out_z = scatter_z(po, zo)

    for copy in gin_z:
        copy.wait_recv()

    def total(buf, got, cols):
        t = buf[place(0), zl, :, cols].astype(F32) + got[0, :, cols].astype(F32)
        return t + got[1, :, cols].astype(F32) + got[2, :, cols].astype(F32)

    dots = jnp.zeros((R, 128), F32)
    for i in range(D // 128):
        cols = slice(i * 128, (i + 1) * 128)
        g = total(px, zx, cols)
        t = x_ref[:, cols].astype(F32)
        gfull[:, cols] = g
        dots = dots + g * gain_ref[i : i + 1, :] * t
    j3.end()
    mean = jnp.sum(dots, axis=1, keepdims=True) * (1.0 / D)
    cubed = inverse * inverse * inverse * mean
    for i in range(D // 128):
        cols = slice(i * 128, (i + 1) * 128)
        t = x_ref[:, cols].astype(F32)
        gin_ref[:, cols] = (
            inverse * (gfull[:, cols] * gain_ref[i : i + 1, :]) - t * cubed
        ).astype(BF16)

    j4.middle()
    j4.end()

    for copy in out_z:
        copy.wait_recv()
    for i in range(D // 128):
        cols = slice(i * 128, (i + 1) * 128)
        out_ref[:, cols] = total(po, zo, cols).astype(BF16)

    ghx.wait_recv()
    gg_ref[...] = gh[0] + gh[1]
    for part in (j1, j2, j3, j4):
        part.finish()
    copies.sent()
    assert (copies.most, copies.count) == (N_SEND, N_RECV), (copies.most, copies.count)


def per_device(inputs, norm_gain, w_up, w_down, grad_out):
    vmem = pl.BlockSpec(memory_space=pltpu.VMEM)
    hbm = pl.BlockSpec(memory_space=pltpu.HBM)
    scratch = [
        ((R, D), BF16), ((D // 128, 128), F32),
        ((D, F), BF16), ((F, D), BF16),
        ((16, R, D), BF16), ((16, R, D), BF16),
        ((T, D), BF16),
        ((H, 2 * T), BF16), ((H, T), BF16), ((2 * T, H), BF16),
        ((T, F), F32), ((T, F), F32),
        ((2 * T, F), BF16), ((T, F), BF16), ((F, 2 * T), BF16),
        ((4, 4, R, D), BF16), ((4, 4, R, D), BF16),
        ((2, 3, 4, R, H), BF16), ((2, 3, 4, R, H), BF16),
        ((3, R, D), BF16), ((3, R, D), BF16),
        ((4, 4, 2, 80, F), BF16), ((4, 2, 3, 80, F), BF16), ((4, 2, 80, F), BF16),
        ((4, 8, 128), F32), ((4, 8, 128), F32),
        ((4, 20, 128), F32), ((4, 20, 128), F32), ((4, 20, 128), F32),
        ((2, 20, 128), F32), ((2, 20, 128), F32),
        ((4, R, D), BF16), ((4, R, 128), F32),
        ((R, D), F32), ((R, 128), F32),
    ]
    out, gin, gup, gdn, gg = pl.pallas_call(
        kernel,
        out_shape=(
            pltpu.VMEM((R, D), BF16),
            pltpu.VMEM((R, D), BF16),
            pltpu.VMEM((D, F), BF16),
            pltpu.VMEM((F, D), BF16),
            pltpu.VMEM((D // 128, 128), F32),
        ),
        in_specs=[hbm] * 5,
        out_specs=(vmem,) * 5,
        scratch_shapes=[pltpu.VMEM(s, t) for s, t in scratch]
        + [
            pltpu.SemaphoreType.DMA((N_SEND,)),
            pltpu.SemaphoreType.DMA((N_RECV,)),
            pltpu.SemaphoreType.DMA((5,)),
        ],
        compiler_params=pltpu.CompilerParams(
            collective_id=0, has_side_effects=True, vmem_limit_bytes=46 << 20
        ),
    )(inputs, norm_gain.reshape(D // 128, 128), w_up, w_down, grad_out)
    return out, gin, gup, gdn, gg.reshape(D)


def solution(mesh):
    return jax.shard_map(
        per_device,
        mesh=mesh,
        in_specs=(
            P(("dp", "tensor"), None),
            P(),
            P(None, "tensor"),
            P("tensor", None),
            P(("dp", "tensor"), None),
        ),
        out_specs=(
            P(("dp", "tensor"), None),
            P(("dp", "tensor"), None),
            P(None, "tensor"),
            P("tensor", None),
            P(),
        ),
        check_vma=False,
    )
```

```python
import functools

import jax
import jax.numpy as jnp
from jax import lax
from jax.experimental import pallas as pl
from jax.experimental.pallas import tpu as pltpu
from jax.sharding import PartitionSpec as P

MESH = pl.DeviceIdType.MESH
F32 = jnp.float32
BF16 = jnp.bfloat16

D = 2560
F = 640
T = 384
R = 24
H = D // 2
N_SEND, N_RECV = 96, 151

SINE = (
    0.9999999958410793,
    -6.579735564529717,
    12.987846451008128,
    -12.207473944175224,
    6.687349899038311,
    -2.367236060103434,
    0.5102235956366108,
)
NT = (((1,), (1,)), ((), ()))
NN = (((1,), (0,)), ((), ()))


def dot(a, b, dims=NN):
    return lax.dot_general(a, b, dims, preferred_element_type=F32)


def staircase(values):
    r = values - jnp.floor(values + 0.5)
    s = r * r
    p = jnp.full_like(s, SINE[-1])
    for c in SINE[-2::-1]:
        p = p * s + c
    return values - p * r


def block_peak(values):
    lane = lax.broadcasted_iota(jnp.int32, values.shape, 1)
    for s in (1, 2, 4, 8):
        up = pltpu.roll(values, s, 1)
        down = pltpu.roll(values, 128 - s, 1)
        values = jnp.maximum(values, jnp.where((lane & s) != 0, up, down))
    return values


def quantize(values, magnitude, floor):
    peak = jnp.maximum(block_peak(magnitude), floor)
    return peak * (1.0 / 6.0) * staircase(values * (6.0 / peak))


class Copies:
    def __init__(self, send, recv):
        self.send, self.recv = send, recv
        self.count, self.spare, self.most, self.open = 0, [], 0, []

    def start(self, src, dst, device):
        if self.spare:
            n = self.spare.pop()
        else:
            n = self.most
            self.most += 1
        copy = pltpu.make_async_remote_copy(
            src_ref=src,
            dst_ref=dst,
            send_sem=self.send.at[n],
            recv_sem=self.recv.at[self.count],
            device_id=device,
            device_id_type=MESH,
        )
        copy.start()
        self.count += 1
        self.open.append((copy, n))
        return copy

    def sent(self, upto=None):
        done = self.open[:upto]
        for copy, n in done:
            copy.wait_send()
            self.spare.append(n)
        self.open = self.open[len(done) :]


def kernel(
    x_hbm, gain_hbm, wu_hbm, wd_hbm, go_hbm,
    out_ref, gin_ref, gup_ref, gdn_ref, gg_ref,
    x_ref, gain_ref, wu, wd, cg, qg, c2, aa, ss, cc, ghq, pa, gz2, hq, ht,
    po, px, ro, rx, zo, zx, w, wr, wz,
    py, pz, gy, gzl, gx, gc, gh, xg, ig, gfull, mx, send, recv, local,
):
    dp, tn = lax.axis_index("dp"), lax.axis_index("tensor")
    zh, x, c = dp // 8, (dp // 2) % 4, dp % 2
    zl, y = tn // 4, tn % 4

    def dev(zh=zh, x=x, c=c, zl=zl, y=y):
        return ((zh * 4 + x) * 2 + c, zl * 4 + y)

    def mod(v):
        return lax.rem(v + 8, 4)

    def place(rel):
        return (rel + 1) % 4

    def block(rel, zz):
        return place(rel) * 4 + zz

    yp, ym = dev(y=mod(y + 1)), dev(y=mod(y - 1))
    xp, xm = dev(x=mod(x + 1)), dev(x=mod(x - 1))
    other = dev(c=1 - c)
    zfar = dev(zh=1 - zh)
    y_peers = [dev(y=mod(y + k)) for k in (1, 2, 3)]
    z_peers = [dev(zl=mod(zl + k)) for k in (1, 2, 3)]
    x_peers = [dev(x=mod(x + k)) for k in (1, 2, 3)]
    copies = Copies(send, recv)
    go = copies.start

    def load(src, dst, n):
        copy = pltpu.make_async_copy(src, dst, local.at[n])
        copy.start()
        return copy

    load_x = load(x_hbm, x_ref, 2)
    load_gain = load(gain_hbm, gain_ref, 3)
    load_own = load(go_hbm, cg.at[block(0, zl)], 4)
    load_up = load(wu_hbm, wu, 0)
    load_down = load(wd_hbm, wd, 1)

    barrier = pltpu.get_barrier_semaphore()
    peers = y_peers + z_peers + x_peers + [other, zfar]
    for peer in peers:
        pl.semaphore_signal(barrier, inc=1, device_id=peer, device_id_type=MESH)
    load_x.wait()
    wide = x_ref[...].astype(F32)
    inverse = lax.rsqrt(jnp.mean(wide * wide, axis=1, keepdims=True) + 1e-05)
    ig[zl] = jnp.broadcast_to(inverse, (R, 128))
    xg[zl] = x_ref[...]
    load_gain.wait()
    pl.semaphore_wait(barrier, len(peers))

    def gather_z(buf, src, k):
        return go(src, buf.at[block(0, zl)], z_peers[k - 1])

    def gather_y(buf, k, src=None):
        zz = mod(zl - k)
        src = buf.at[block(0, zz)] if src is None else src
        return go(src, buf.at[block(-1, zz)], yp), go(src, buf.at[block(1, zz)], ym)

    def forward(buf, k, pair):
        plus, minus = pair
        zz = mod(zl - k)
        left, right = (slice(None), pl.ds(0, H)), (slice(None), pl.ds(H, H))
        plus.wait_recv()
        a = go(buf.at[(block(-1, zz), *left)], buf.at[(block(2, zz), *left)], yp)
        minus.wait_recv()
        b = go(buf.at[(block(1, zz), *right)], buf.at[(block(2, zz), *right)], ym)
        return a, b

    cy, qy, cz, qz, cf, qf = {}, {}, {}, {}, [], []
    cy[0] = gather_y(cg, 0, go_hbm)
    cz[1] = gather_z(cg, go_hbm, 1)

    for i in range(D // 128):
        cols = slice(i * 128, (i + 1) * 128)
        normed = wide[:, cols] * inverse * gain_ref[i : i + 1, :]
        q = quantize(normed, jnp.abs(normed), 1.5)
        qg[block(0, zl), :, cols] = q.astype(BF16)

    mine = qg.at[block(0, zl)]
    qy[0] = gather_y(qg, 0)
    qz[1] = gather_z(qg, mine, 1)
    qz[3] = gather_z(qg, mine, 3)

    def next_q(k):
        qz[k].wait_recv()
        qy[k] = gather_y(qg, k)

    def next_c(k):
        cz[k].wait_recv()
        cy[k] = gather_y(cg, k)

    def forward_q(k):
        qf.extend(forward(qg, k, qy[k]))

    def forward_c(k):
        cf.extend(forward(cg, k, cy[k]))

    next_c(1)
    forward_c(0)
    forward_q(0)
    next_q(1)
    qz[2] = gather_z(qg, mine, 2)
    next_q(3)
    cz[3] = gather_z(cg, go_hbm, 3)
    forward_q(1)
    next_q(2)
    cz[2] = gather_z(cg, go_hbm, 2)
    forward_q(3)
    forward_c(1)
    next_c(3)
    forward_q(2)
    next_c(2)
    xz = [go(x_ref, xg.at[zl], peer) for peer in z_peers]
    xz += [go(ig.at[zl], ig.at[zl], peer) for peer in z_peers]

    load_up.wait()
    near, last = (0, 12), (12, 4)

    def pre_group(group, most):
        b, n = group
        rows = slice(b * R, (b + n) * R)

        @pl.loop(0, 5)
        def _(i):
            ks = pl.ds(pl.multiple_of(i * 512, 512), 512)
            v = qg[b : b + n, :, ks].astype(F32).reshape(n * R, 512).astype(BF16)
            part = dot(v, wu[ks, :])

            @pl.when(i == 0)
            def _():
                pa[rows, :] = part

            @pl.when(i > 0)
            def _():
                pa[rows, :] += part

        @pl.loop(0, n)
        def _(i):
            at = pl.ds(pl.multiple_of(b * R + i * R, R), R)
            top = jnp.zeros((R, 128), F32)
            for j in range(F // 128):
                cols = slice(j * 128, (j + 1) * 128)
                active = jnp.maximum(pa[at, cols], 0.0)
                pa[at, cols] = active
                top = jnp.maximum(top, active)
            most[...] = jnp.maximum(most[...], top)

    mx[...] = jnp.zeros((R, 128), F32)
    pre_group(near, mx)
    for copy in qf:
        copy.wait_recv()
    forward_c(3)
    pre_group(last, mx)
    most = jnp.max(jnp.max(mx[...], axis=0, keepdims=True), axis=1, keepdims=True)
    py[y] = jnp.broadcast_to(most * most, (8, 128))
    pyx = [go(py.at[y], py.at[y], peer) for peer in y_peers]
    forward_c(2)

    def lay(i, start, put):
        cols = pl.ds(pl.multiple_of(start + i * 256, 256), 256)
        v = qg[:, :, cols].astype(F32).reshape(T, 256)
        put(pl.ds(pl.multiple_of(i * 256, 256), 256), v.T.astype(BF16))

    def put_other(rows, v):
        ss[rows, :] = v

    def put_own(rows, v):
        aa[rows, pl.ds(0, T)] = v

    @pl.loop(0, 5)
    def _(i):
        lay(i, (1 - c) * H, put_other)

    aax = go(ss, aa.at[:, pl.ds(T, T)], other)

    load_down.wait()
    other_half = pl.ds(pl.multiple_of((1 - c) * H, H), H)
    own_half = pl.ds(pl.multiple_of(c * H, H), H)
    gzx, ccx = [], []

    def grad_group(group):
        b, n = group
        rows = slice(b * R, (b + n) * R)

        @pl.loop(0, 5)
        def _(i):
            ks = pl.ds(pl.multiple_of(i * 512, 512), 512)
            v = cg[b : b + n, :, ks].astype(F32).reshape(n * R, 512).astype(BF16)
            c2[rows, ks] = v
            part = dot(v, wd[:, ks], NT)

            @pl.when(i == 0)
            def _():
                ghq[rows, :] = part

            @pl.when(i > 0)
            def _():
                ghq[rows, :] += part

        @pl.loop(0, n // 2)
        def _(i):
            at = pl.ds(pl.multiple_of(b * R + i * 2 * R, 2 * R), 2 * R)
            for j in range(F // 128):
                cols = slice(j * 128, (j + 1) * 128)
                gz2[at, cols] = (ghq[at, cols] * 2.0 * pa[at, cols]).astype(BF16)

        far = slice(T + b * R, T + (b + n) * R)
        gzx.append(go(gz2.at[rows], gz2.at[far], other))
        ccx.append(go(c2.at[rows, other_half], cc.at[far], other))

    load_own.wait()
    grad_group(near)

    for copy in pyx:
        copy.wait_recv()
    peak = jnp.maximum(jnp.maximum(py[0], py[1]), jnp.maximum(py[2], py[3]))
    pz[zl] = peak
    pzx = [go(pz.at[zl], pz.at[zl], peer) for peer in z_peers]
    for copy in cf:
        copy.wait_recv()
    grad_group(last)

    @pl.loop(0, 5)
    def _(i):
        lay(i, c * H, put_own)


    class Ring:
        def __init__(self, plus, minus, view, got, tiles, cut):
            self.to = (plus, minus)
            self.view, self.got, self.tiles, self.cut = view, got, tiles, cut
            self.last = [None, None]

        def send(self, s, way):
            at = self.view(-1 - s if way == 0 else 1 + s, way)
            self.last[way] = go(at, self.got.at[way, s], self.to[way])

        def take(self, s):
            for way in (0, 1):
                self.last[way].wait_recv()
                mine = self.view(-2 - s if way == 0 else 2 + s, way)
                theirs = self.got.at[way, s]

                @pl.loop(0, self.tiles)
                def _(i):
                    at = self.cut(i)
                    both = mine[at].astype(F32) + theirs[at].astype(F32)
                    mine[at] = both.astype(BF16)

                if s < 2:
                    self.send(s + 1, way)

    class Part:
        def __init__(self, n, buf, where):
            self.n, self.buf, self.where = n, buf, where
            self.ring = Ring(
                xp, xm, lambda rel, way: w.at[n, mod(x + rel), way], wr.at[n], 5,
                lambda i: pl.ds(pl.multiple_of(i * 16, 16), 16),
            )

        def cross_z(self):
            self.far = [go(w.at[self.n, x], wz.at[self.n], zfar)]

        def begin(self):
            for copy in self.far:
                copy.wait_recv()
            for way in (0, 1):
                both = w[self.n, x, way].astype(F32) + wz[self.n, way].astype(F32)
                self.buf[self.where(c, x, way)] = both.astype(BF16)
            at = self.buf.at[self.where(c, x)]
            self.plus, self.minus = go(at, at, xp), go(at, at, xm)
            self.cross = [go(at, at, other)]

        def middle(self):
            self.plus.wait_recv()
            at = self.buf.at[self.where(c, mod(x - 1), 0)]
            self.fplus = go(at, at, xp)
            at = self.buf.at[self.where(c, mod(x - 1))]
            self.cross.append(go(at, at, other))
            self.minus.wait_recv()
            at = self.buf.at[self.where(c, mod(x + 1), 1)]
            self.fminus = go(at, at, xm)
            at = self.buf.at[self.where(c, mod(x + 1))]
            self.cross.append(go(at, at, other))

        def end(self):
            self.fplus.wait_recv()
            at = self.buf.at[self.where(c, mod(x + 2), 0)]
            self.cross.append(go(at, at, other))
            self.fminus.wait_recv()
            at = self.buf.at[self.where(c, mod(x + 2), 1)]
            self.cross.append(go(at, at, other))

        def finish(self):
            for copy in self.cross:
                copy.wait_recv()

    class First(Part):
        def __init__(self, *args):
            super().__init__(*args)
            self.got, self.far = [None, None], []

        def send(self, half):
            self.got[half] = [
                go(w.at[self.n, mod(x + k), half], wr.at[self.n, half, k - 1], x_peers[k - 1])
                for k in (1, 3, 2)
            ]

        def take(self, half):
            for copy in self.got[half]:
                copy.wait_recv()
            mine, got = w.at[self.n, x, half], wr.at[self.n, half]

            @pl.loop(0, 5)
            def _(i):
                at = pl.ds(pl.multiple_of(i * 16, 16), 16)
                t = mine[at].astype(F32) + got[0, at].astype(F32)
                t = t + got[1, at].astype(F32) + got[2, at].astype(F32)
                mine[at] = t.astype(BF16)

            self.far.append(go(mine, wz.at[self.n, half], zfar))

    def up_rows(p):
        def where(core, j, way=None):
            start = core * H + j * 320 + p * 160 + (0 if way is None else way * 80)
            n = 160 if way is None else 80
            return (pl.ds(pl.multiple_of(start, n), n), slice(None))

        return where

    def down_rows(p):
        def where(core, j, way=None):
            cols = pl.ds(pl.multiple_of(core * H + p * F, 128), F)
            start = j * 160 + (0 if way is None else way * 80)
            n = 160 if way is None else 80
            return (pl.ds(pl.multiple_of(start, n), n), cols)

        return where

    j1, j2 = First(0, gup_ref, up_rows(0)), First(1, gup_ref, up_rows(1))
    j3, j4 = Part(2, gdn_ref, down_rows(0)), Part(3, gdn_ref, down_rows(1))

    def p_view(buf):
        return lambda rel, way: buf.at[place(rel), :, :, pl.ds(way * H, H)]

    out = Ring(yp, ym, p_view(po), ro, 4, lambda i: i)
    gin = Ring(yp, ym, p_view(px), rx, 4, lambda i: i)

    aax.wait_recv()
    for copy in gzx:
        copy.wait_recv()

    def up_chunk(p, j):
        rows = pl.ds(pl.multiple_of(j * 320 + p * 160, 160), 160)
        w[p, j] = dot(aa[rows, :], gz2[...]).reshape(2, 80, F).astype(BF16)

    mark = len(copies.open)
    def up_half(half):
        for k in (1, 3, 2, 0):
            j = mod(x + k)
            rows = pl.ds(pl.multiple_of(j * 320 + half * 80, 16), 80)
            w[0, j, half] = dot(aa[rows, :], gz2[...]).astype(BF16)

    up_half(0)
    j1.send(0)
    up_half(1)
    j1.send(1)

    @pl.loop(0, 5)
    def _(i):
        ns = pl.ds(pl.multiple_of(i * 512, 512), 512)
        part = dot(gz2[pl.ds(0, T), :], wu[ns, :], NT)
        px[:, :, :, ns] = part.reshape(4, 4, R, 512).astype(BF16)

    gin.send(0, 0)
    gin.send(0, 1)
    for k in (1, 3, 2):
        up_chunk(1, mod(x + k))
    j2.send(0)
    j2.send(1)

    for copy in pzx:
        copy.wait_recv()
    peak = jnp.maximum(jnp.maximum(pz[0], pz[1]), jnp.maximum(pz[2], pz[3]))
    floor = ((peak[0:1, :] + 1e-06) * 0.125).reshape(1, 1, 128)

    def hidden_tile(i):
        rows = slice(i * 128, (i + 1) * 128)

        @pl.loop(0, F // 128)
        def _(j):
            cols = pl.ds(pl.multiple_of(j * 128, 128), 128)
            active = pa[rows, cols]
            hidden = (active * active).T.reshape(8, 16, 128)
            most = jnp.maximum(jnp.max(hidden, axis=1, keepdims=True), floor)
            q = most * (1.0 / 6.0) * staircase(hidden * (6.0 / most))
            q = q.reshape(128, 128)
            ht[cols, rows] = q.astype(BF16)
            hq[rows, cols] = q.T.astype(BF16)

    hidden_tile(0)
    hidden_tile(1)
    j1.take(0)
    hidden_tile(2)
    htx = go(ht.at[:, pl.ds(0, T)], ht.at[:, pl.ds(T, T)], other)

    def down_chunk(j):
        rows = pl.ds(pl.multiple_of(j * 160, 160), 160)
        for p in (0, 1):
            part = dot(ht[rows, :], cc[:, p * F : (p + 1) * F])
            w[2 + p, j] = part.reshape(2, 80, F).astype(BF16)

    up_chunk(1, x)
    cc[pl.ds(0, T), :] = c2[:, own_half]
    copies.sent(mark)
    gin.take(0)
    for copy in ccx:
        copy.wait_recv()
    htx.wait_recv()
    down_chunk(mod(x - 1))
    j3.ring.send(0, 0)
    down_chunk(mod(x + 1))
    j3.ring.send(0, 1)
    j1.take(1)
    j4.ring.send(0, 0)
    j4.ring.send(0, 1)
    down_chunk(mod(x + 2))
    down_chunk(x)

    def out_tile(i):
        ns = slice(i * 512, (i + 1) * 512)
        part = dot(hq[...], wd[:, ns])
        po[:, :, :, ns] = part.reshape(4, 4, R, 512).astype(BF16)

    out_tile(0)
    j2.take(0)
    out_tile(1)
    gin.take(1)
    out_tile(2)
    out_tile(3)
    out_tile(4)
    out.send(0, 0)
    out.send(0, 1)

    class ScatterZ:
        def __init__(self, buf, got):
            self.buf, self.got = buf.at[place(0)], got
            near = zl + 1 - 2 * lax.rem(zl, 2)
            self.across = mod(zl + 2)
            self.near = [
                go(self.buf.at[mod(near + 2)], got.at[1], dev(zl=near)),
                go(self.buf.at[near], got.at[0], dev(zl=near)),
            ]

        def middle(self):
            self.near[0].wait_recv()
            mine = self.buf.at[self.across]

            @pl.loop(0, 5)
            def _(i):
                cols = pl.ds(pl.multiple_of(i * 512, 512), 512)
                t = mine[:, cols].astype(F32) + self.got[1, :, cols].astype(F32)
                mine[:, cols] = t.astype(BF16)

            self.far = go(mine, self.got.at[2], dev(zl=self.across))

        def end(self):
            self.near[1].wait_recv()
            self.far.wait_recv()

        def total(self, cols):
            t = self.buf[zl, :, cols].astype(F32) + self.got[0, :, cols].astype(F32)
            return t + self.got[2, :, cols].astype(F32)

    j2.take(1)
    j3.ring.take(0)
    j4.ring.take(0)
    gin.take(2)

    for copy in xz:
        copy.wait_recv()
    for i in range(D // 128):
        cols = slice(i * 128, (i + 1) * 128)
        t = jnp.zeros((R, 128), F32)
        for k in range(4):
            g = px[place(0), k, :, cols].astype(F32)
            t = t + g * xg[k, :, cols].astype(F32) * ig[k]
        gzl[zl, i : i + 1, :] = jnp.sum(t, axis=0, keepdims=True)
    gain_copies = [go(gzl.at[zl], gzl.at[zl], peer) for peer in z_peers]
    gin_z = ScatterZ(px, zx)

    def gain_sum(parts, n, nxt, at, to):
        for copy in gain_copies:
            copy.wait_recv()
        t = parts[0]
        for k in range(1, n):
            t = t + parts[k]
        if nxt is not None:
            nxt[at] = t
            gain_copies[:] = [go(nxt.at[at], nxt.at[at], peer) for peer in to]
        return t

    j3.ring.take(1)
    j1.begin()
    out.take(0)
    j4.ring.take(1)
    j3.ring.take(2)
    j3.cross_z()
    j1.middle()
    j4.ring.take(2)
    j4.cross_z()
    j2.begin()
    j1.end()
    out.take(1)
    gain_sum(gzl, 4, gy, y, y_peers)
    gin_z.middle()
    j2.middle()
    out.take(2)
    j3.begin()
    gain_sum(gy, 4, gx, x, x_peers)
    j2.end()
    j4.begin()
    out_z = ScatterZ(po, zo)
    j3.middle()
    gain_sum(gx, 4, gc, c, [other])
    j3.end()
    gain_sum(gc, 2, gh, zh, [zfar])
    j4.middle()
    out_z.middle()

    gin_z.end()

    dots = jnp.zeros((R, 128), F32)
    for i in range(D // 128):
        cols = slice(i * 128, (i + 1) * 128)
        g = gin_z.total(cols)
        t = x_ref[:, cols].astype(F32)
        gfull[:, cols] = g
        dots = dots + g * gain_ref[i : i + 1, :] * t
    mean = jnp.sum(dots, axis=1, keepdims=True) * (1.0 / D)
    cubed = inverse * inverse * inverse * mean
    for i in range(D // 128):
        cols = slice(i * 128, (i + 1) * 128)
        t = x_ref[:, cols].astype(F32)
        gin_ref[:, cols] = (
            inverse * (gfull[:, cols] * gain_ref[i : i + 1, :]) - t * cubed
        ).astype(BF16)

    j4.end()

    out_z.end()
    for i in range(D // 128):
        cols = slice(i * 128, (i + 1) * 128)
        out_ref[:, cols] = out_z.total(cols).astype(BF16)

    gg_ref[...] = gain_sum(gh, 2, None, None, None)
    for part in (j1, j2, j3, j4):
        part.finish()
    copies.sent()
    assert (copies.most, copies.count) == (N_SEND, N_RECV), (copies.most, copies.count)


def per_device(inputs, norm_gain, w_up, w_down, grad_out):
    vmem = pl.BlockSpec(memory_space=pltpu.VMEM)
    hbm = pl.BlockSpec(memory_space=pltpu.HBM)
    scratch = [
        ((R, D), BF16), ((D // 128, 128), F32),
        ((D, F), BF16), ((F, D), BF16),
        ((16, R, D), BF16), ((16, R, D), BF16),
        ((T, D), BF16),
        ((H, 2 * T), BF16), ((H, T), BF16), ((2 * T, H), BF16),
        ((T, F), F32), ((T, F), F32),
        ((2 * T, F), BF16), ((T, F), BF16), ((F, 2 * T), BF16),
        ((4, 4, R, D), BF16), ((4, 4, R, D), BF16),
        ((2, 3, 4, R, H), BF16), ((2, 3, 4, R, H), BF16),
        ((3, R, D), BF16), ((3, R, D), BF16),
        ((4, 4, 2, 80, F), BF16), ((4, 2, 3, 80, F), BF16), ((4, 2, 80, F), BF16),
        ((4, 8, 128), F32), ((4, 8, 128), F32),
        ((4, 20, 128), F32), ((4, 20, 128), F32), ((4, 20, 128), F32),
        ((2, 20, 128), F32), ((2, 20, 128), F32),
        ((4, R, D), BF16), ((4, R, 128), F32),
        ((R, D), F32), ((R, 128), F32),
    ]
    shapes = [(R, D), (R, D), (D, F), (F, D), (D // 128, 128)]
    types = [BF16, BF16, BF16, BF16, F32]
    out, gin, gup, gdn, gg = pl.pallas_call(
        kernel,
        out_shape=[pltpu.VMEM(s, t) for s, t in zip(shapes, types, strict=True)],
        in_specs=[hbm] * 5,
        out_specs=[vmem] * 5,
        scratch_shapes=[pltpu.VMEM(s, t) for s, t in scratch]
        + [
            pltpu.SemaphoreType.DMA((N_SEND,)),
            pltpu.SemaphoreType.DMA((N_RECV,)),
            pltpu.SemaphoreType.DMA((5,)),
        ],
        compiler_params=pltpu.CompilerParams(
            collective_id=0, has_side_effects=True, vmem_limit_bytes=46 << 20
        ),
    )(inputs, norm_gain.reshape(D // 128, 128), w_up, w_down, grad_out)
    return out, gin, gup, gdn, gg.reshape(D)


def solution(mesh):
    return jax.shard_map(
        per_device,
        mesh=mesh,
        in_specs=(
            P(("dp", "tensor"), None),
            P(),
            P(None, "tensor"),
            P("tensor", None),
            P(("dp", "tensor"), None),
        ),
        out_specs=(
            P(("dp", "tensor"), None),
            P(("dp", "tensor"), None),
            P(None, "tensor"),
            P("tensor", None),
            P(),
        ),
        check_vma=False,
    )
```

```python
import functools

import jax
import jax.numpy as jnp
from jax import lax
from jax.experimental import pallas as pl
from jax.experimental.pallas import tpu as pltpu
from jax.sharding import PartitionSpec as P

MESH = pl.DeviceIdType.MESH
F32 = jnp.float32
BF16 = jnp.bfloat16

D = 2560
F = 640
T = 384
R = 24
H = D // 2
N_SEND, N_RECV = 96, 151

SINE = (
    0.9999999958410793,
    -6.579735564529717,
    12.987846451008128,
    -12.207473944175224,
    6.687349899038311,
    -2.367236060103434,
    0.5102235956366108,
)
NT = (((1,), (1,)), ((), ()))
NN = (((1,), (0,)), ((), ()))


def dot(a, b, dims=NN):
    return lax.dot_general(a, b, dims, preferred_element_type=F32)


def staircase(values):
    r = values - jnp.floor(values + 0.5)
    s = r * r
    p = jnp.full_like(s, SINE[-1])
    for c in SINE[-2::-1]:
        p = p * s + c
    return values - p * r


def block_peak(values):
    lane = lax.broadcasted_iota(jnp.int32, values.shape, 1)
    for s in (1, 2, 4, 8):
        up = pltpu.roll(values, s, 1)
        down = pltpu.roll(values, 128 - s, 1)
        values = jnp.maximum(values, jnp.where((lane & s) != 0, up, down))
    return values


def quantize(values, magnitude, floor):
    peak = jnp.maximum(block_peak(magnitude), floor)
    return peak * (1.0 / 6.0) * staircase(values * (6.0 / peak))


class Copies:
    def __init__(self, send, recv):
        self.send, self.recv = send, recv
        self.count, self.spare, self.most, self.open = 0, [], 0, []

    def start(self, src, dst, device):
        if self.spare:
            n = self.spare.pop()
        else:
            n = self.most
            self.most += 1
        copy = pltpu.make_async_remote_copy(
            src_ref=src,
            dst_ref=dst,
            send_sem=self.send.at[n],
            recv_sem=self.recv.at[self.count],
            device_id=device,
            device_id_type=MESH,
        )
        copy.start()
        self.count += 1
        self.open.append((copy, n))
        return copy

    def sent(self, upto=None):
        done = self.open[:upto]
        for copy, n in done:
            copy.wait_send()
            self.spare.append(n)
        self.open = self.open[len(done) :]


def kernel(
    x_hbm, gain_hbm, wu_hbm, wd_hbm, go_hbm,
    out_ref, gin_ref, gup_ref, gdn_ref, gg_ref,
    x_ref, gain_ref, wu, wd, cg, qg, c2, aa, ss, cc, ghq, pa, gz2, hq, ht,
    po, px, ro, rx, zo, zx, w, wr, wz,
    py, pz, gy, gzl, gx, gc, gh, xg, ig, gfull, mx, send, recv, local,
):
    dp, tn = lax.axis_index("dp"), lax.axis_index("tensor")
    zh, x, c = dp // 8, (dp // 2) % 4, dp % 2
    zl, y = tn // 4, tn % 4

    def dev(zh=zh, x=x, c=c, zl=zl, y=y):
        return ((zh * 4 + x) * 2 + c, zl * 4 + y)

    def mod(v):
        return lax.rem(v + 8, 4)

    def place(rel):
        return (rel + 1) % 4

    def block(rel, zz):
        return place(rel) * 4 + zz

    yp, ym = dev(y=mod(y + 1)), dev(y=mod(y - 1))
    xp, xm = dev(x=mod(x + 1)), dev(x=mod(x - 1))
    other = dev(c=1 - c)
    zfar = dev(zh=1 - zh)
    y_peers = [dev(y=mod(y + k)) for k in (1, 2, 3)]
    z_peers = [dev(zl=mod(zl + k)) for k in (1, 2, 3)]
    x_peers = [dev(x=mod(x + k)) for k in (1, 2, 3)]
    copies = Copies(send, recv)
    go = copies.start

    def load(src, dst, n):
        copy = pltpu.make_async_copy(src, dst, local.at[n])
        copy.start()
        return copy

    load_x = load(x_hbm, x_ref, 2)
    load_gain = load(gain_hbm, gain_ref, 3)
    load_own = load(go_hbm, cg.at[block(0, zl)], 4)
    load_up = load(wu_hbm, wu, 0)
    load_down = load(wd_hbm, wd, 1)

    barrier = pltpu.get_barrier_semaphore()
    peers = y_peers + z_peers + x_peers + [other, zfar]
    for peer in peers:
        pl.semaphore_signal(barrier, inc=1, device_id=peer, device_id_type=MESH)
    load_x.wait()
    wide = x_ref[...].astype(F32)
    inverse = lax.rsqrt(jnp.mean(wide * wide, axis=1, keepdims=True) + 1e-05)
    ig[zl] = jnp.broadcast_to(inverse, (R, 128))
    xg[zl] = x_ref[...]
    load_gain.wait()
    pl.semaphore_wait(barrier, len(peers))

    def gather_z(buf, src, k):
        return go(src, buf.at[block(0, zl)], z_peers[k - 1])

    def gather_y(buf, k, src=None):
        zz = mod(zl - k)
        src = buf.at[block(0, zz)] if src is None else src
        return go(src, buf.at[block(-1, zz)], yp), go(src, buf.at[block(1, zz)], ym)

    def forward(buf, k, pair):
        plus, minus = pair
        zz = mod(zl - k)
        left, right = (slice(None), pl.ds(0, H)), (slice(None), pl.ds(H, H))
        plus.wait_recv()
        a = go(buf.at[(block(-1, zz), *left)], buf.at[(block(2, zz), *left)], yp)
        minus.wait_recv()
        b = go(buf.at[(block(1, zz), *right)], buf.at[(block(2, zz), *right)], ym)
        return a, b

    cy, qy, cz, qz, cf, qf = {}, {}, {}, {}, [], []
    cy[0] = gather_y(cg, 0, go_hbm)
    cz[1] = gather_z(cg, go_hbm, 1)

    for i in range(D // 128):
        cols = slice(i * 128, (i + 1) * 128)
        normed = wide[:, cols] * inverse * gain_ref[i : i + 1, :]
        q = quantize(normed, jnp.abs(normed), 1.5)
        qg[block(0, zl), :, cols] = q.astype(BF16)

    mine = qg.at[block(0, zl)]
    qy[0] = gather_y(qg, 0)
    qz[1] = gather_z(qg, mine, 1)
    qz[3] = gather_z(qg, mine, 3)

    def next_q(k):
        qz[k].wait_recv()
        qy[k] = gather_y(qg, k)

    def next_c(k):
        cz[k].wait_recv()
        cy[k] = gather_y(cg, k)

    def forward_q(k):
        qf.extend(forward(qg, k, qy[k]))

    def forward_c(k):
        cf.extend(forward(cg, k, cy[k]))

    next_c(1)
    forward_c(0)
    forward_q(0)
    next_q(1)
    qz[2] = gather_z(qg, mine, 2)
    next_q(3)
    cz[3] = gather_z(cg, go_hbm, 3)
    forward_q(1)
    next_q(2)
    cz[2] = gather_z(cg, go_hbm, 2)
    forward_q(3)
    forward_c(1)
    next_c(3)
    forward_q(2)
    next_c(2)
    xz = [go(x_ref, xg.at[zl], peer) for peer in z_peers]
    xz += [go(ig.at[zl], ig.at[zl], peer) for peer in z_peers]

    load_up.wait()
    near, last = (0, 12), (12, 4)

    def pre_group(group, most):
        b, n = group
        rows = slice(b * R, (b + n) * R)

        @pl.loop(0, 5)
        def _(i):
            ks = pl.ds(pl.multiple_of(i * 512, 512), 512)
            v = qg[b : b + n, :, ks].astype(F32).reshape(n * R, 512).astype(BF16)
            part = dot(v, wu[ks, :])

            @pl.when(i == 0)
            def _():
                pa[rows, :] = part

            @pl.when(i > 0)
            def _():
                pa[rows, :] += part

        @pl.loop(0, n)
        def _(i):
            at = pl.ds(pl.multiple_of(b * R + i * R, R), R)
            top = jnp.zeros((R, 128), F32)
            for j in range(F // 128):
                cols = slice(j * 128, (j + 1) * 128)
                active = jnp.maximum(pa[at, cols], 0.0)
                pa[at, cols] = active
                top = jnp.maximum(top, active)
            most[...] = jnp.maximum(most[...], top)

    mx[...] = jnp.zeros((R, 128), F32)
    pre_group(near, mx)
    for copy in qf:
        copy.wait_recv()
    forward_c(3)
    pre_group(last, mx)
    most = jnp.max(jnp.max(mx[...], axis=0, keepdims=True), axis=1, keepdims=True)
    py[y] = jnp.broadcast_to(most * most, (8, 128))
    pyx = [go(py.at[y], py.at[y], peer) for peer in y_peers]
    forward_c(2)

    def lay(i, start, put):
        cols = pl.ds(pl.multiple_of(start + i * 256, 256), 256)
        v = qg[:, :, cols].astype(F32).reshape(T, 256)
        put(pl.ds(pl.multiple_of(i * 256, 256), 256), v.T.astype(BF16))

    def put_other(rows, v):
        ss[rows, :] = v

    def put_own(rows, v):
        aa[rows, pl.ds(0, T)] = v

    @pl.loop(0, 5)
    def _(i):
        lay(i, (1 - c) * H, put_other)

    aax = go(ss, aa.at[:, pl.ds(T, T)], other)

    load_down.wait()
    other_half = pl.ds(pl.multiple_of((1 - c) * H, H), H)
    own_half = pl.ds(pl.multiple_of(c * H, H), H)
    gzx, ccx = [], []

    def grad_group(group):
        b, n = group
        rows = slice(b * R, (b + n) * R)

        @pl.loop(0, 5)
        def _(i):
            ks = pl.ds(pl.multiple_of(i * 512, 512), 512)
            v = cg[b : b + n, :, ks].astype(F32).reshape(n * R, 512).astype(BF16)
            c2[rows, ks] = v
            part = dot(v, wd[:, ks], NT)

            @pl.when(i == 0)
            def _():
                ghq[rows, :] = part

            @pl.when(i > 0)
            def _():
                ghq[rows, :] += part

        @pl.loop(0, n // 2)
        def _(i):
            at = pl.ds(pl.multiple_of(b * R + i * 2 * R, 2 * R), 2 * R)
            for j in range(F // 128):
                cols = slice(j * 128, (j + 1) * 128)
                gz2[at, cols] = (ghq[at, cols] * 2.0 * pa[at, cols]).astype(BF16)

        far = slice(T + b * R, T + (b + n) * R)
        gzx.append(go(gz2.at[rows], gz2.at[far], other))
        ccx.append(go(c2.at[rows, other_half], cc.at[far], other))

    load_own.wait()
    grad_group(near)

    for copy in pyx:
        copy.wait_recv()
    peak = jnp.maximum(jnp.maximum(py[0], py[1]), jnp.maximum(py[2], py[3]))
    pz[zl] = peak
    pzx = [go(pz.at[zl], pz.at[zl], peer) for peer in z_peers]
    for copy in cf:
        copy.wait_recv()
    grad_group(last)

    @pl.loop(0, 5)
    def _(i):
        lay(i, c * H, put_own)


    class Ring:
        def __init__(self, plus, minus, view, got, tiles, cut):
            self.to = (plus, minus)
            self.view, self.got, self.tiles, self.cut = view, got, tiles, cut
            self.last = [None, None]

        def send(self, s, way):
            at = self.view(-1 - s if way == 0 else 1 + s, way)
            self.last[way] = go(at, self.got.at[way, s], self.to[way])

        def take(self, s):
            for way in (0, 1):
                self.last[way].wait_recv()
                mine = self.view(-2 - s if way == 0 else 2 + s, way)
                theirs = self.got.at[way, s]

                @pl.loop(0, self.tiles)
                def _(i):
                    at = self.cut(i)
                    both = mine[at].astype(F32) + theirs[at].astype(F32)
                    mine[at] = both.astype(BF16)

                if s < 2:
                    self.send(s + 1, way)

    class Part:
        def __init__(self, n, buf, where):
            self.n, self.buf, self.where = n, buf, where
            self.ring = Ring(
                xp, xm, lambda rel, way: w.at[n, mod(x + rel), way], wr.at[n], 5,
                lambda i: pl.ds(pl.multiple_of(i * 16, 16), 16),
            )

        def cross_z(self):
            self.far = [go(w.at[self.n, x], wz.at[self.n], zfar)]

        def begin(self):
            for copy in self.far:
                copy.wait_recv()
            for way in (0, 1):
                both = w[self.n, x, way].astype(F32) + wz[self.n, way].astype(F32)
                self.buf[self.where(c, x, way)] = both.astype(BF16)
            at = self.buf.at[self.where(c, x)]
            self.plus, self.minus = go(at, at, xp), go(at, at, xm)
            self.cross = [go(at, at, other)]

        def middle(self):
            self.plus.wait_recv()
            at = self.buf.at[self.where(c, mod(x - 1), 0)]
            self.fplus = go(at, at, xp)
            at = self.buf.at[self.where(c, mod(x - 1))]
            self.cross.append(go(at, at, other))
            self.minus.wait_recv()
            at = self.buf.at[self.where(c, mod(x + 1), 1)]
            self.fminus = go(at, at, xm)
            at = self.buf.at[self.where(c, mod(x + 1))]
            self.cross.append(go(at, at, other))

        def end(self):
            self.fplus.wait_recv()
            at = self.buf.at[self.where(c, mod(x + 2), 0)]
            self.cross.append(go(at, at, other))
            self.fminus.wait_recv()
            at = self.buf.at[self.where(c, mod(x + 2), 1)]
            self.cross.append(go(at, at, other))

        def finish(self):
            for copy in self.cross:
                copy.wait_recv()

    class First(Part):
        def __init__(self, *args):
            super().__init__(*args)
            self.got, self.far = [None, None], []

        def send(self, half):
            self.got[half] = [
                go(w.at[self.n, mod(x + k), half], wr.at[self.n, half, k - 1], x_peers[k - 1])
                for k in (1, 3, 2)
            ]

        def take(self, half):
            for copy in self.got[half]:
                copy.wait_recv()
            mine, got = w.at[self.n, x, half], wr.at[self.n, half]

            @pl.loop(0, 5)
            def _(i):
                at = pl.ds(pl.multiple_of(i * 16, 16), 16)
                t = mine[at].astype(F32) + got[0, at].astype(F32)
                t = t + got[1, at].astype(F32) + got[2, at].astype(F32)
                mine[at] = t.astype(BF16)

            self.far.append(go(mine, wz.at[self.n, half], zfar))

    def up_rows(p):
        def where(core, j, way=None):
            start = core * H + j * 320 + p * 160 + (0 if way is None else way * 80)
            n = 160 if way is None else 80
            return (pl.ds(pl.multiple_of(start, n), n), slice(None))

        return where

    def down_rows(p):
        def where(core, j, way=None):
            cols = pl.ds(pl.multiple_of(core * H + p * F, 128), F)
            start = j * 160 + (0 if way is None else way * 80)
            n = 160 if way is None else 80
            return (pl.ds(pl.multiple_of(start, n), n), cols)

        return where

    j1, j2 = First(0, gup_ref, up_rows(0)), First(1, gup_ref, up_rows(1))
    j3, j4 = Part(2, gdn_ref, down_rows(0)), Part(3, gdn_ref, down_rows(1))

    def p_view(buf):
        return lambda rel, way: buf.at[place(rel), :, :, pl.ds(way * H, H)]

    out = Ring(yp, ym, p_view(po), ro, 4, lambda i: i)
    gin = Ring(yp, ym, p_view(px), rx, 4, lambda i: i)

    aax.wait_recv()
    for copy in gzx:
        copy.wait_recv()

    def up_chunk(p, j):
        rows = pl.ds(pl.multiple_of(j * 320 + p * 160, 160), 160)
        w[p, j] = dot(aa[rows, :], gz2[...]).reshape(2, 80, F).astype(BF16)

    mark = len(copies.open)
    def up_half(half):
        for k in (1, 3, 2, 0):
            j = mod(x + k)
            rows = pl.ds(pl.multiple_of(j * 320 + half * 80, 16), 80)
            w[0, j, half] = dot(aa[rows, :], gz2[...]).astype(BF16)

    up_half(0)
    j1.send(0)
    up_half(1)
    j1.send(1)

    @pl.loop(0, 5)
    def _(i):
        ns = pl.ds(pl.multiple_of(i * 512, 512), 512)
        part = dot(gz2[pl.ds(0, T), :], wu[ns, :], NT)
        px[:, :, :, ns] = part.reshape(4, 4, R, 512).astype(BF16)

    gin.send(0, 0)
    gin.send(0, 1)
    for k in (1, 3, 2):
        up_chunk(1, mod(x + k))
    j2.send(0)
    j2.send(1)

    for copy in pzx:
        copy.wait_recv()
    peak = jnp.maximum(jnp.maximum(pz[0], pz[1]), jnp.maximum(pz[2], pz[3]))
    floor = ((peak[0:1, :] + 1e-06) * 0.125).reshape(1, 1, 128)

    def hidden_tile(i):
        rows = slice(i * 128, (i + 1) * 128)

        @pl.loop(0, F // 128)
        def _(j):
            cols = pl.ds(pl.multiple_of(j * 128, 128), 128)
            active = pa[rows, cols]
            hidden = (active * active).T.reshape(8, 16, 128)
            most = jnp.maximum(jnp.max(hidden, axis=1, keepdims=True), floor)
            q = most * (1.0 / 6.0) * staircase(hidden * (6.0 / most))
            q = q.reshape(128, 128)
            ht[cols, rows] = q.astype(BF16)
            hq[rows, cols] = q.T.astype(BF16)

    hidden_tile(0)
    hidden_tile(1)
    j1.take(0)
    hidden_tile(2)
    htx = go(ht.at[:, pl.ds(0, T)], ht.at[:, pl.ds(T, T)], other)

    def down_chunk(j):
        rows = pl.ds(pl.multiple_of(j * 160, 160), 160)
        for p in (0, 1):
            part = dot(ht[rows, :], cc[:, p * F : (p + 1) * F])
            w[2 + p, j] = part.reshape(2, 80, F).astype(BF16)

    up_chunk(1, x)
    cc[pl.ds(0, T), :] = c2[:, own_half]
    copies.sent(mark)
    gin.take(0)
    for copy in ccx:
        copy.wait_recv()
    htx.wait_recv()
    down_chunk(mod(x - 1))
    j3.ring.send(0, 0)
    down_chunk(mod(x + 1))
    j3.ring.send(0, 1)
    j1.take(1)
    j4.ring.send(0, 0)
    j4.ring.send(0, 1)
    down_chunk(mod(x + 2))
    down_chunk(x)

    def out_tile(i):
        ns = slice(i * 512, (i + 1) * 512)
        part = dot(hq[...], wd[:, ns])
        po[:, :, :, ns] = part.reshape(4, 4, R, 512).astype(BF16)

    out_tile(0)
    j2.take(0)
    out_tile(1)
    gin.take(1)
    out_tile(2)
    out_tile(3)
    out_tile(4)
    out.send(0, 0)
    out.send(0, 1)

    class ScatterZ:
        def __init__(self, buf, got):
            self.buf, self.got = buf.at[place(0)], got
            near = zl + 1 - 2 * lax.rem(zl, 2)
            self.across = mod(zl + 2)
            self.near = [
                go(self.buf.at[mod(near + 2)], got.at[1], dev(zl=near)),
                go(self.buf.at[near], got.at[0], dev(zl=near)),
            ]

        def middle(self):
            self.near[0].wait_recv()
            mine = self.buf.at[self.across]

            @pl.loop(0, 5)
            def _(i):
                cols = pl.ds(pl.multiple_of(i * 512, 512), 512)
                t = mine[:, cols].astype(F32) + self.got[1, :, cols].astype(F32)
                mine[:, cols] = t.astype(BF16)

            self.far = go(mine, self.got.at[2], dev(zl=self.across))

        def end(self):
            self.near[1].wait_recv()
            self.far.wait_recv()

        def total(self, cols):
            t = self.buf[zl, :, cols].astype(F32) + self.got[0, :, cols].astype(F32)
            return t + self.got[2, :, cols].astype(F32)

    j2.take(1)
    j3.ring.take(0)
    j4.ring.take(0)
    gin.take(2)

    for copy in xz:
        copy.wait_recv()
    for i in range(D // 128):
        cols = slice(i * 128, (i + 1) * 128)
        t = jnp.zeros((R, 128), F32)
        for k in range(4):
            g = px[place(0), k, :, cols].astype(F32)
            t = t + g * xg[k, :, cols].astype(F32) * ig[k]
        gzl[zl, i : i + 1, :] = jnp.sum(t, axis=0, keepdims=True)
    gain_copies = [go(gzl.at[zl], gzl.at[zl], peer) for peer in z_peers]
    gin_z = ScatterZ(px, zx)

    def gain_sum(parts, n, nxt, at, to):
        for copy in gain_copies:
            copy.wait_recv()
        t = parts[0]
        for k in range(1, n):
            t = t + parts[k]
        if nxt is not None:
            nxt[at] = t
            gain_copies[:] = [go(nxt.at[at], nxt.at[at], peer) for peer in to]
        return t

    j3.ring.take(1)
    j1.begin()
    out.take(0)
    j4.ring.take(1)
    j3.ring.take(2)
    j3.cross_z()
    j1.middle()
    j4.ring.take(2)
    j4.cross_z()
    j2.begin()
    j1.end()
    out.take(1)
    gain_sum(gzl, 4, gy, y, y_peers)
    gin_z.middle()
    j2.middle()
    out.take(2)
    j3.begin()
    gain_sum(gy, 4, gx, x, x_peers)
    j2.end()
    j4.begin()
    out_z = ScatterZ(po, zo)
    j3.middle()
    gain_sum(gx, 4, gc, c, [other])
    j3.end()
    gain_sum(gc, 2, gh, zh, [zfar])
    j4.middle()
    out_z.middle()

    gin_z.end()

    dots = jnp.zeros((R, 128), F32)
    for i in range(D // 128):
        cols = slice(i * 128, (i + 1) * 128)
        g = gin_z.total(cols)
        t = x_ref[:, cols].astype(F32)
        gfull[:, cols] = g
        dots = dots + g * gain_ref[i : i + 1, :] * t
    mean = jnp.sum(dots, axis=1, keepdims=True) * (1.0 / D)
    cubed = inverse * inverse * inverse * mean
    for i in range(D // 128):
        cols = slice(i * 128, (i + 1) * 128)
        t = x_ref[:, cols].astype(F32)
        gin_ref[:, cols] = (
            inverse * (gfull[:, cols] * gain_ref[i : i + 1, :]) - t * cubed
        ).astype(BF16)

    j4.end()

    out_z.end()
    for i in range(D // 128):
        cols = slice(i * 128, (i + 1) * 128)
        out_ref[:, cols] = out_z.total(cols).astype(BF16)

    gg_ref[...] = gain_sum(gh, 2, None, None, None)
    for part in (j1, j2, j3, j4):
        part.finish()
    copies.sent()
    assert (copies.most, copies.count) == (N_SEND, N_RECV), (copies.most, copies.count)


def per_device(inputs, norm_gain, w_up, w_down, grad_out):
    vmem = pl.BlockSpec(memory_space=pltpu.VMEM)
    hbm = pl.BlockSpec(memory_space=pltpu.HBM)
    scratch = [
        ((R, D), BF16), ((D // 128, 128), F32),
        ((D, F), BF16), ((F, D), BF16),
        ((16, R, D), BF16), ((16, R, D), BF16),
        ((T, D), BF16),
        ((H, 2 * T), BF16), ((H, T), BF16), ((2 * T, H), BF16),
        ((T, F), F32), ((T, F), F32),
        ((2 * T, F), BF16), ((T, F), BF16), ((F, 2 * T), BF16),
        ((4, 4, R, D), BF16), ((4, 4, R, D), BF16),
        ((2, 3, 4, R, H), BF16), ((2, 3, 4, R, H), BF16),
        ((3, R, D), BF16), ((3, R, D), BF16),
        ((4, 4, 2, 80, F), BF16), ((4, 2, 3, 80, F), BF16), ((4, 2, 80, F), BF16),
        ((4, 8, 128), F32), ((4, 8, 128), F32),
        ((4, 20, 128), F32), ((4, 20, 128), F32), ((4, 20, 128), F32),
        ((2, 20, 128), F32), ((2, 20, 128), F32),
        ((4, R, D), BF16), ((4, R, 128), F32),
        ((R, D), F32), ((R, 128), F32),
    ]
    shapes = [(R, D), (R, D), (D, F), (F, D), (D // 128, 128)]
    types = [BF16, BF16, BF16, BF16, F32]
    out, gin, gup, gdn, gg = pl.pallas_call(
        kernel,
        out_shape=[pltpu.VMEM(s, t) for s, t in zip(shapes, types, strict=True)],
        in_specs=[hbm] * 5,
        out_specs=[vmem] * 5,
        scratch_shapes=[pltpu.VMEM(s, t) for s, t in scratch]
        + [
            pltpu.SemaphoreType.DMA((N_SEND,)),
            pltpu.SemaphoreType.DMA((N_RECV,)),
            pltpu.SemaphoreType.DMA((5,)),
        ],
        compiler_params=pltpu.CompilerParams(
            collective_id=0, has_side_effects=True, vmem_limit_bytes=60231680
        ),
    )(inputs, norm_gain.reshape(D // 128, 128), w_up, w_down, grad_out)
    return out, gin, gup, gdn, gg.reshape(D)


def solution(mesh):
    return jax.shard_map(
        per_device,
        mesh=mesh,
        in_specs=(
            P(("dp", "tensor"), None),
            P(),
            P(None, "tensor"),
            P("tensor", None),
            P(("dp", "tensor"), None),
        ),
        out_specs=(
            P(("dp", "tensor"), None),
            P(("dp", "tensor"), None),
            P(None, "tensor"),
            P("tensor", None),
            P(),
        ),
        check_vma=False,
    )
```

```python
import functools

import jax
import jax.numpy as jnp
from jax import lax
from jax.experimental import pallas as pl
from jax.experimental.pallas import tpu as pltpu
from jax.sharding import PartitionSpec as P

MESH = pl.DeviceIdType.MESH
F32 = jnp.float32
BF16 = jnp.bfloat16

D = 2560
F = 640
T = 384
R = 24
H = D // 2
N_SEND, N_RECV = 96, 151

SINE = (
    0.9999999958410793,
    -6.579735564529717,
    12.987846451008128,
    -12.207473944175224,
    6.687349899038311,
    -2.367236060103434,
    0.5102235956366108,
)
NT = (((1,), (1,)), ((), ()))
NN = (((1,), (0,)), ((), ()))


def dot(a, b, dims=NN):
    return lax.dot_general(a, b, dims, preferred_element_type=F32)


def staircase(values):
    r = values - jnp.floor(values + 0.5)
    s = r * r
    p = jnp.full_like(s, SINE[-1])
    for c in SINE[-2::-1]:
        p = p * s + c
    return values - p * r


def block_peak(values):
    lane = lax.broadcasted_iota(jnp.int32, values.shape, 1)
    for s in (1, 2, 4, 8):
        up = pltpu.roll(values, s, 1)
        down = pltpu.roll(values, 128 - s, 1)
        values = jnp.maximum(values, jnp.where((lane & s) != 0, up, down))
    return values


def quantize(values, magnitude, floor):
    peak = jnp.maximum(block_peak(magnitude), floor)
    return peak * (1.0 / 6.0) * staircase(values * (6.0 / peak))


class Copies:
    def __init__(self, send, recv):
        self.send, self.recv = send, recv
        self.count, self.spare, self.most, self.open = 0, [], 0, []

    def start(self, src, dst, device):
        if self.spare:
            n = self.spare.pop()
        else:
            n = self.most
            self.most += 1
        copy = pltpu.make_async_remote_copy(
            src_ref=src,
            dst_ref=dst,
            send_sem=self.send.at[n],
            recv_sem=self.recv.at[self.count],
            device_id=device,
            device_id_type=MESH,
        )
        copy.start()
        self.count += 1
        self.open.append((copy, n))
        return copy

    def sent(self, upto=None):
        done = self.open[:upto]
        for copy, n in done:
            copy.wait_send()
            self.spare.append(n)
        self.open = self.open[len(done) :]


def kernel(
    x_hbm, gain_hbm, wu_hbm, wd_hbm, go_hbm,
    out_ref, gin_ref, gup_ref, gdn_ref, gg_ref,
    x_ref, gain_ref, wu, wd, cg, qg, c2, aa, ss, cc, ghq, pa, gz2, hq, ht,
    po, px, ro, rx, zo, zx, w, wr, wz,
    py, pz, gy, gzl, gx, gc, gh, xg, ig, gfull, mx, send, recv, local,
):
    dp, tn = lax.axis_index("dp"), lax.axis_index("tensor")
    zh, x, c = dp // 8, (dp // 2) % 4, dp % 2
    zl, y = tn // 4, tn % 4

    def dev(zh=zh, x=x, c=c, zl=zl, y=y):
        return ((zh * 4 + x) * 2 + c, zl * 4 + y)

    def mod(v):
        return lax.rem(v + 8, 4)

    def place(rel):
        return (rel + 1) % 4

    def block(rel, zz):
        return place(rel) * 4 + zz

    yp, ym = dev(y=mod(y + 1)), dev(y=mod(y - 1))
    xp, xm = dev(x=mod(x + 1)), dev(x=mod(x - 1))
    other = dev(c=1 - c)
    zfar = dev(zh=1 - zh)
    y_peers = [dev(y=mod(y + k)) for k in (1, 2, 3)]
    z_peers = [dev(zl=mod(zl + k)) for k in (1, 2, 3)]
    x_peers = [dev(x=mod(x + k)) for k in (1, 2, 3)]
    copies = Copies(send, recv)
    go = copies.start

    def load(src, dst, n):
        copy = pltpu.make_async_copy(src, dst, local.at[n])
        copy.start()
        return copy

    load_x = load(x_hbm, x_ref, 2)
    load_gain = load(gain_hbm, gain_ref, 3)
    load_own = load(go_hbm, cg.at[block(0, zl)], 4)
    load_up = load(wu_hbm, wu, 0)
    load_down = load(wd_hbm, wd, 1)

    barrier = pltpu.get_barrier_semaphore()
    peers = y_peers + z_peers + x_peers + [other, zfar]
    for peer in peers:
        pl.semaphore_signal(barrier, inc=1, device_id=peer, device_id_type=MESH)
    load_x.wait()
    wide = x_ref[...].astype(F32)
    inverse = lax.rsqrt(jnp.mean(wide * wide, axis=1, keepdims=True) + 1e-05)
    ig[zl] = jnp.broadcast_to(inverse, (R, 128))
    xg[zl] = x_ref[...]
    load_gain.wait()
    pl.semaphore_wait(barrier, len(peers))

    def gather_z(buf, src, k):
        return go(src, buf.at[block(0, zl)], z_peers[k - 1])

    def gather_y(buf, k, src=None):
        zz = mod(zl - k)
        src = buf.at[block(0, zz)] if src is None else src
        return go(src, buf.at[block(-1, zz)], yp), go(src, buf.at[block(1, zz)], ym)

    def forward(buf, k, pair):
        plus, minus = pair
        zz = mod(zl - k)
        left, right = (slice(None), pl.ds(0, H)), (slice(None), pl.ds(H, H))
        plus.wait_recv()
        a = go(buf.at[(block(-1, zz), *left)], buf.at[(block(2, zz), *left)], yp)
        minus.wait_recv()
        b = go(buf.at[(block(1, zz), *right)], buf.at[(block(2, zz), *right)], ym)
        return a, b

    cy, qy, cz, qz, cf, qf = {}, {}, {}, {}, [], []
    cy[0] = gather_y(cg, 0, go_hbm)
    cz[1] = gather_z(cg, go_hbm, 1)

    for i in range(D // 128):
        cols = slice(i * 128, (i + 1) * 128)
        normed = wide[:, cols] * inverse * gain_ref[i : i + 1, :]
        q = quantize(normed, jnp.abs(normed), 1.5)
        qg[block(0, zl), :, cols] = q.astype(BF16)

    mine = qg.at[block(0, zl)]
    qy[0] = gather_y(qg, 0)
    qz[1] = gather_z(qg, mine, 1)
    qz[3] = gather_z(qg, mine, 3)

    def next_q(k):
        qz[k].wait_recv()
        qy[k] = gather_y(qg, k)

    def next_c(k):
        cz[k].wait_recv()
        cy[k] = gather_y(cg, k)

    def forward_q(k):
        qf.extend(forward(qg, k, qy[k]))

    def forward_c(k):
        cf.extend(forward(cg, k, cy[k]))

    next_c(1)
    forward_c(0)
    forward_q(0)
    next_q(1)
    qz[2] = gather_z(qg, mine, 2)
    next_q(3)
    cz[3] = gather_z(cg, go_hbm, 3)
    forward_q(1)
    next_q(2)
    cz[2] = gather_z(cg, go_hbm, 2)
    forward_q(3)
    forward_c(1)
    next_c(3)
    forward_q(2)
    next_c(2)
    xz = [go(x_ref, xg.at[zl], peer) for peer in z_peers]
    xz += [go(ig.at[zl], ig.at[zl], peer) for peer in z_peers]

    load_up.wait()
    near, last = (0, 12), (12, 4)

    def pre_group(group, most):
        b, n = group
        rows = slice(b * R, (b + n) * R)

        @pl.loop(0, 5)
        def _(i):
            ks = pl.ds(pl.multiple_of(i * 512, 512), 512)
            v = qg[b : b + n, :, ks].astype(F32).reshape(n * R, 512).astype(BF16)
            part = dot(v, wu[ks, :])

            @pl.when(i == 0)
            def _():
                pa[rows, :] = part

            @pl.when(i > 0)
            def _():
                pa[rows, :] += part

        @pl.loop(0, n)
        def _(i):
            at = pl.ds(pl.multiple_of(b * R + i * R, R), R)
            top = jnp.zeros((R, 128), F32)
            for j in range(F // 128):
                cols = slice(j * 128, (j + 1) * 128)
                active = jnp.maximum(pa[at, cols], 0.0)
                pa[at, cols] = active
                top = jnp.maximum(top, active)
            most[...] = jnp.maximum(most[...], top)

    mx[...] = jnp.zeros((R, 128), F32)
    pre_group(near, mx)

    def lay(part, far):
        blocks = slice(0, 11) if part == 0 else slice(10, 16)
        keep = slice(0, 256) if part == 0 else slice(16, 144)
        lanes = slice(0, 256) if part == 0 else slice(256, T)
        start = (1 - c) * H if far else c * H

        @pl.loop(0, 5)
        def _(i):
            cols = pl.ds(pl.multiple_of(start + i * 256, 256), 256)
            rows = pl.ds(pl.multiple_of(i * 256, 256), 256)
            v = qg[blocks, :, cols].astype(F32).reshape(-1, 256)[keep].T.astype(BF16)
            if far:
                ss[rows, lanes] = v
            else:
                aa[rows, lanes] = v

    lay(0, True)
    lay(0, False)
    for copy in qf:
        copy.wait_recv()
    forward_c(3)
    pre_group(last, mx)
    most = jnp.max(jnp.max(mx[...], axis=0, keepdims=True), axis=1, keepdims=True)
    py[y] = jnp.broadcast_to(most * most, (8, 128))
    pyx = [go(py.at[y], py.at[y], peer) for peer in y_peers]
    forward_c(2)

    lay(1, True)
    aax = go(ss, aa.at[:, pl.ds(T, T)], other)

    load_down.wait()
    other_half = pl.ds(pl.multiple_of((1 - c) * H, H), H)
    own_half = pl.ds(pl.multiple_of(c * H, H), H)
    gzx, ccx = [], []

    def grad_group(group):
        b, n = group
        rows = slice(b * R, (b + n) * R)

        @pl.loop(0, 5)
        def _(i):
            ks = pl.ds(pl.multiple_of(i * 512, 512), 512)
            v = cg[b : b + n, :, ks].astype(F32).reshape(n * R, 512).astype(BF16)
            c2[rows, ks] = v
            part = dot(v, wd[:, ks], NT)

            @pl.when(i == 0)
            def _():
                ghq[rows, :] = part

            @pl.when(i > 0)
            def _():
                ghq[rows, :] += part

        @pl.loop(0, n // 2)
        def _(i):
            at = pl.ds(pl.multiple_of(b * R + i * 2 * R, 2 * R), 2 * R)
            for j in range(F // 128):
                cols = slice(j * 128, (j + 1) * 128)
                gz2[at, cols] = (ghq[at, cols] * 2.0 * pa[at, cols]).astype(BF16)

        far = slice(T + b * R, T + (b + n) * R)
        gzx.append(go(gz2.at[rows], gz2.at[far], other))
        ccx.append(go(c2.at[rows, other_half], cc.at[far], other))

    load_own.wait()
    grad_group(near)

    for copy in pyx:
        copy.wait_recv()
    peak = jnp.maximum(jnp.maximum(py[0], py[1]), jnp.maximum(py[2], py[3]))
    pz[zl] = peak
    pzx = [go(pz.at[zl], pz.at[zl], peer) for peer in z_peers]
    for copy in cf:
        copy.wait_recv()
    grad_group(last)

    lay(1, False)


    class Ring:
        def __init__(self, plus, minus, view, got, tiles, cut):
            self.to = (plus, minus)
            self.view, self.got, self.tiles, self.cut = view, got, tiles, cut
            self.last = [None, None]

        def send(self, s, way):
            at = self.view(-1 - s if way == 0 else 1 + s, way)
            self.last[way] = go(at, self.got.at[way, s], self.to[way])

        def take(self, s):
            for way in (0, 1):
                self.last[way].wait_recv()
                mine = self.view(-2 - s if way == 0 else 2 + s, way)
                theirs = self.got.at[way, s]

                @pl.loop(0, self.tiles)
                def _(i):
                    at = self.cut(i)
                    both = mine[at].astype(F32) + theirs[at].astype(F32)
                    mine[at] = both.astype(BF16)

                if s < 2:
                    self.send(s + 1, way)

    class Part:
        def __init__(self, n, buf, where):
            self.n, self.buf, self.where = n, buf, where
            self.ring = Ring(
                xp, xm, lambda rel, way: w.at[n, mod(x + rel), way], wr.at[n], 5,
                lambda i: pl.ds(pl.multiple_of(i * 16, 16), 16),
            )

        def cross_z(self):
            self.far = [go(w.at[self.n, x], wz.at[self.n], zfar)]

        def begin(self):
            for copy in self.far:
                copy.wait_recv()
            for way in (0, 1):
                both = w[self.n, x, way].astype(F32) + wz[self.n, way].astype(F32)
                self.buf[self.where(c, x, way)] = both.astype(BF16)
            at = self.buf.at[self.where(c, x)]
            self.plus, self.minus = go(at, at, xp), go(at, at, xm)
            self.cross = [go(at, at, other)]

        def middle(self):
            self.plus.wait_recv()
            at = self.buf.at[self.where(c, mod(x - 1), 0)]
            self.fplus = go(at, at, xp)
            at = self.buf.at[self.where(c, mod(x - 1))]
            self.cross.append(go(at, at, other))
            self.minus.wait_recv()
            at = self.buf.at[self.where(c, mod(x + 1), 1)]
            self.fminus = go(at, at, xm)
            at = self.buf.at[self.where(c, mod(x + 1))]
            self.cross.append(go(at, at, other))

        def end(self):
            self.fplus.wait_recv()
            at = self.buf.at[self.where(c, mod(x + 2), 0)]
            self.cross.append(go(at, at, other))
            self.fminus.wait_recv()
            at = self.buf.at[self.where(c, mod(x + 2), 1)]
            self.cross.append(go(at, at, other))

        def finish(self):
            for copy in self.cross:
                copy.wait_recv()

    class First(Part):
        def __init__(self, *args):
            super().__init__(*args)
            self.got, self.far = [None, None], []

        def send(self, half):
            self.got[half] = [
                go(w.at[self.n, mod(x + k), half], wr.at[self.n, half, k - 1], x_peers[k - 1])
                for k in (1, 3, 2)
            ]

        def take(self, half):
            for copy in self.got[half]:
                copy.wait_recv()
            mine, got = w.at[self.n, x, half], wr.at[self.n, half]

            @pl.loop(0, 5)
            def _(i):
                at = pl.ds(pl.multiple_of(i * 16, 16), 16)
                t = mine[at].astype(F32) + got[0, at].astype(F32)
                t = t + got[1, at].astype(F32) + got[2, at].astype(F32)
                mine[at] = t.astype(BF16)

            self.far.append(go(mine, wz.at[self.n, half], zfar))

    def up_rows(p):
        def where(core, j, way=None):
            start = core * H + j * 320 + p * 160 + (0 if way is None else way * 80)
            n = 160 if way is None else 80
            return (pl.ds(pl.multiple_of(start, n), n), slice(None))

        return where

    def down_rows(p):
        def where(core, j, way=None):
            cols = pl.ds(pl.multiple_of(core * H + p * F, 128), F)
            start = j * 160 + (0 if way is None else way * 80)
            n = 160 if way is None else 80
            return (pl.ds(pl.multiple_of(start, n), n), cols)

        return where

    j1, j2 = First(0, gup_ref, up_rows(0)), First(1, gup_ref, up_rows(1))
    j3, j4 = Part(2, gdn_ref, down_rows(0)), Part(3, gdn_ref, down_rows(1))

    def p_view(buf):
        return lambda rel, way: buf.at[place(rel), :, :, pl.ds(way * H, H)]

    out = Ring(yp, ym, p_view(po), ro, 4, lambda i: i)
    gin = Ring(yp, ym, p_view(px), rx, 4, lambda i: i)

    aax.wait_recv()
    for copy in gzx:
        copy.wait_recv()

    def up_chunk(p, j):
        rows = pl.ds(pl.multiple_of(j * 320 + p * 160, 160), 160)
        w[p, j] = dot(aa[rows, :], gz2[...]).reshape(2, 80, F).astype(BF16)

    mark = len(copies.open)
    def up_half(half):
        for k in (1, 3, 2, 0):
            j = mod(x + k)
            rows = pl.ds(pl.multiple_of(j * 320 + half * 80, 16), 80)
            w[0, j, half] = dot(aa[rows, :], gz2[...]).astype(BF16)

    up_half(0)
    j1.send(0)
    up_half(1)
    j1.send(1)

    @pl.loop(0, 5)
    def _(i):
        ns = pl.ds(pl.multiple_of(i * 512, 512), 512)
        part = dot(gz2[pl.ds(0, T), :], wu[ns, :], NT)
        px[:, :, :, ns] = part.reshape(4, 4, R, 512).astype(BF16)

    gin.send(0, 0)
    gin.send(0, 1)
    for k in (1, 3, 2):
        up_chunk(1, mod(x + k))
    j2.send(0)
    j2.send(1)

    for copy in pzx:
        copy.wait_recv()
    peak = jnp.maximum(jnp.maximum(pz[0], pz[1]), jnp.maximum(pz[2], pz[3]))
    floor = ((peak[0:1, :] + 1e-06) * 0.125).reshape(1, 1, 128)

    def hidden_tile(i):
        rows = slice(i * 128, (i + 1) * 128)

        @pl.loop(0, F // 128)
        def _(j):
            cols = pl.ds(pl.multiple_of(j * 128, 128), 128)
            active = pa[rows, cols]
            hidden = (active * active).T.reshape(8, 16, 128)
            most = jnp.maximum(jnp.max(hidden, axis=1, keepdims=True), floor)
            q = most * (1.0 / 6.0) * staircase(hidden * (6.0 / most))
            q = q.reshape(128, 128)
            ht[cols, rows] = q.astype(BF16)
            hq[rows, cols] = q.T.astype(BF16)

    hidden_tile(0)
    hidden_tile(1)
    j1.take(0)
    hidden_tile(2)
    htx = go(ht.at[:, pl.ds(0, T)], ht.at[:, pl.ds(T, T)], other)

    def down_chunk(j):
        rows = pl.ds(pl.multiple_of(j * 160, 160), 160)
        for p in (0, 1):
            part = dot(ht[rows, :], cc[:, p * F : (p + 1) * F])
            w[2 + p, j] = part.reshape(2, 80, F).astype(BF16)

    up_chunk(1, x)
    cc[pl.ds(0, T), :] = c2[:, own_half]
    copies.sent(mark)
    gin.take(0)
    for copy in ccx:
        copy.wait_recv()
    htx.wait_recv()
    down_chunk(mod(x - 1))
    j3.ring.send(0, 0)
    down_chunk(mod(x + 1))
    j3.ring.send(0, 1)
    j1.take(1)
    j4.ring.send(0, 0)
    j4.ring.send(0, 1)
    down_chunk(mod(x + 2))
    down_chunk(x)

    def out_tile(i):
        ns = slice(i * 512, (i + 1) * 512)
        part = dot(hq[...], wd[:, ns])
        po[:, :, :, ns] = part.reshape(4, 4, R, 512).astype(BF16)

    out_tile(0)
    j2.take(0)
    out_tile(1)
    gin.take(1)
    out_tile(2)
    out_tile(3)
    out_tile(4)
    out.send(0, 0)
    out.send(0, 1)

    class ScatterZ:
        def __init__(self, buf, got):
            self.buf, self.got = buf.at[place(0)], got
            near = zl + 1 - 2 * lax.rem(zl, 2)
            self.across = mod(zl + 2)
            self.near = [
                go(self.buf.at[mod(near + 2)], got.at[1], dev(zl=near)),
                go(self.buf.at[near], got.at[0], dev(zl=near)),
            ]

        def middle(self):
            self.near[0].wait_recv()
            mine = self.buf.at[self.across]

            @pl.loop(0, 5)
            def _(i):
                cols = pl.ds(pl.multiple_of(i * 512, 512), 512)
                t = mine[:, cols].astype(F32) + self.got[1, :, cols].astype(F32)
                mine[:, cols] = t.astype(BF16)

            self.far = go(mine, self.got.at[2], dev(zl=self.across))

        def end(self):
            self.near[1].wait_recv()
            self.far.wait_recv()

        def total(self, cols):
            t = self.buf[zl, :, cols].astype(F32) + self.got[0, :, cols].astype(F32)
            return t + self.got[2, :, cols].astype(F32)

    j2.take(1)
    j3.ring.take(0)
    j4.ring.take(0)
    gin.take(2)

    for copy in xz:
        copy.wait_recv()
    for i in range(D // 128):
        cols = slice(i * 128, (i + 1) * 128)
        t = jnp.zeros((R, 128), F32)
        for k in range(4):
            g = px[place(0), k, :, cols].astype(F32)
            t = t + g * xg[k, :, cols].astype(F32) * ig[k]
        gzl[zl, i : i + 1, :] = jnp.sum(t, axis=0, keepdims=True)
    gain_copies = [go(gzl.at[zl], gzl.at[zl], peer) for peer in z_peers]
    gin_z = ScatterZ(px, zx)

    def gain_sum(parts, n, nxt, at, to):
        for copy in gain_copies:
            copy.wait_recv()
        t = parts[0]
        for k in range(1, n):
            t = t + parts[k]
        if nxt is not None:
            nxt[at] = t
            gain_copies[:] = [go(nxt.at[at], nxt.at[at], peer) for peer in to]
        return t

    j3.ring.take(1)
    j1.begin()
    out.take(0)
    j4.ring.take(1)
    j3.ring.take(2)
    j3.cross_z()
    j1.middle()
    j4.ring.take(2)
    j4.cross_z()
    j2.begin()
    j1.end()
    out.take(1)
    gain_sum(gzl, 4, gy, y, y_peers)
    gin_z.middle()
    j2.middle()
    out.take(2)
    j3.begin()
    gain_sum(gy, 4, gx, x, x_peers)
    j2.end()
    j4.begin()
    out_z = ScatterZ(po, zo)
    j3.middle()
    gain_sum(gx, 4, gc, c, [other])
    j4.middle()
    gain_sum(gc, 2, gh, zh, [zfar])
    out_z.middle()
    j3.end()

    gin_z.end()

    dots = jnp.zeros((R, 128), F32)
    for i in range(D // 128):
        cols = slice(i * 128, (i + 1) * 128)
        g = gin_z.total(cols)
        t = x_ref[:, cols].astype(F32)
        gfull[:, cols] = g
        dots = dots + g * gain_ref[i : i + 1, :] * t
    mean = jnp.sum(dots, axis=1, keepdims=True) * (1.0 / D)
    cubed = inverse * inverse * inverse * mean
    for i in range(D // 128):
        cols = slice(i * 128, (i + 1) * 128)
        t = x_ref[:, cols].astype(F32)
        gin_ref[:, cols] = (
            inverse * (gfull[:, cols] * gain_ref[i : i + 1, :]) - t * cubed
        ).astype(BF16)

    j4.end()

    out_z.end()
    for i in range(D // 128):
        cols = slice(i * 128, (i + 1) * 128)
        out_ref[:, cols] = out_z.total(cols).astype(BF16)

    gg_ref[...] = gain_sum(gh, 2, None, None, None)
    for part in (j1, j2, j3, j4):
        part.finish()
    copies.sent()
    assert (copies.most, copies.count) == (N_SEND, N_RECV), (copies.most, copies.count)


def per_device(inputs, norm_gain, w_up, w_down, grad_out):
    vmem = pl.BlockSpec(memory_space=pltpu.VMEM)
    hbm = pl.BlockSpec(memory_space=pltpu.HBM)
    scratch = [
        ((R, D), BF16), ((D // 128, 128), F32),
        ((D, F), BF16), ((F, D), BF16),
        ((16, R, D), BF16), ((16, R, D), BF16),
        ((T, D), BF16),
        ((H, 2 * T), BF16), ((H, T), BF16), ((2 * T, H), BF16),
        ((T, F), F32), ((T, F), F32),
        ((2 * T, F), BF16), ((T, F), BF16), ((F, 2 * T), BF16),
        ((4, 4, R, D), BF16), ((4, 4, R, D), BF16),
        ((2, 3, 4, R, H), BF16), ((2, 3, 4, R, H), BF16),
        ((3, R, D), BF16), ((3, R, D), BF16),
        ((4, 4, 2, 80, F), BF16), ((4, 2, 3, 80, F), BF16), ((4, 2, 80, F), BF16),
        ((4, 8, 128), F32), ((4, 8, 128), F32),
        ((4, 20, 128), F32), ((4, 20, 128), F32), ((4, 20, 128), F32),
        ((2, 20, 128), F32), ((2, 20, 128), F32),
        ((4, R, D), BF16), ((4, R, 128), F32),
        ((R, D), F32), ((R, 128), F32),
    ]
    shapes = [(R, D), (R, D), (D, F), (F, D), (D // 128, 128)]
    types = [BF16, BF16, BF16, BF16, F32]
    out, gin, gup, gdn, gg = pl.pallas_call(
        kernel,
        out_shape=[pltpu.VMEM(s, t) for s, t in zip(shapes, types, strict=True)],
        in_specs=[hbm] * 5,
        out_specs=[vmem] * 5,
        scratch_shapes=[pltpu.VMEM(s, t) for s, t in scratch]
        + [
            pltpu.SemaphoreType.DMA((N_SEND,)),
            pltpu.SemaphoreType.DMA((N_RECV,)),
            pltpu.SemaphoreType.DMA((5,)),
        ],
        compiler_params=pltpu.CompilerParams(
            collective_id=0, has_side_effects=True, vmem_limit_bytes=60231680
        ),
    )(inputs, norm_gain.reshape(D // 128, 128), w_up, w_down, grad_out)
    return out, gin, gup, gdn, gg.reshape(D)


def solution(mesh):
    return jax.shard_map(
        per_device,
        mesh=mesh,
        in_specs=(
            P(("dp", "tensor"), None),
            P(),
            P(None, "tensor"),
            P("tensor", None),
            P(("dp", "tensor"), None),
        ),
        out_specs=(
            P(("dp", "tensor"), None),
            P(("dp", "tensor"), None),
            P(None, "tensor"),
            P("tensor", None),
            P(),
        ),
        check_vma=False,
    )
```
